256 devices in a mesh: img: 16 (over z, y_hi), txt: 16 (over y_lo, x, core).
Axes of the slice: x: 4, y: 4 (y_hi: 2, y_lo: 2; y = y_hi * 2 + y_lo), z: 8, core: 2. Of those that a mesh axis runs over, the one named last changes fastest.
Arguments:
- image_emb: bfloat16 [16384, 1152], P(('img', 'txt')), may hold values from -6 to 6
- text_emb: bfloat16 [16384, 1152], P(('txt', 'img')), may hold values from -6 to 6
- positive: int32 [16384], P('img'), may hold values from 0 to 16383, each once
- loss_scale: float32 [], replicated, may hold values from 256 to 1024
Outputs:
- grad_image: bfloat16 [16384, 1152], P(('img', 'txt'))
- grad_text: bfloat16 [16384, 1152], P(('txt', 'img'))
The draws below stay inside these ranges and needn't reach their ends.
Inputs may be any that keep to these rules, and one draw needn't show every extreme that they name: `positive`: every text is the pair of exactly one image.
All inputs are finite; a program needn't handle non-finite values.
Results may differ from the reference program's by a relative error of at most 0.0088.
Values may be sent and summed in bfloat16 or wider, within the bound.
No kernel may reach another device: no remote copies, remote signals or barrier semaphores. Data moves between devices by JAX's collectives and lax.ppermute only.
A program may use at most 64 MiB of HBM per device.

```python
import math
import jax
import jax.numpy as jnp
from jax import lax

D = 1152
IMG_DEV = 1024
IMAGES = 16384
TEXTS = 16384


def block_levels(rng, dims, split, smallest, high):
    def one(axis_at, blocks):
        draws = jax.random.uniform(jax.random.fold_in(jax.random.fold_in(rng, 6), axis_at), (blocks,), jnp.float32, smallest / len(split), high / len(split))
        return jnp.repeat(jnp.exp(draws), dims[axis_at] // blocks).reshape((-1,) + (1,) * (len(dims) - axis_at - 1))

    loudness = one(*split[0])
    for cut in split[1:]:
        loudness = loudness * one(*cut)
    return loudness


def normal_values(own_key, dims, spread, most, split=(), kind=jnp.bfloat16):
    level = block_levels(own_key, dims, split, -0.22, 0.18) if split else 1.0
    values = jax.random.normal(own_key, dims, jnp.float32) * spread * level
    return jnp.minimum(jnp.maximum(values, -most), most).astype(kind)


def setup_inputs(seed: int = 0) -> dict:
    seeds = jax.random.split(jax.random.key(seed), 5)
    image_emb = normal_values(seeds[0], (IMAGES, D), 1.0, 6.0, ((0, 256),))
    text_emb = normal_values(seeds[1], (TEXTS, D), 1.0, 6.0, ((0, 256),))
    positive = jax.random.permutation(seeds[2], TEXTS).astype(jnp.int32)
    loss_scale = jnp.clip(jnp.exp(jax.random.uniform(seeds[3], (), jnp.float32, math.log(256.0), math.log(1024.0))), 256.0, 1024.0)
    return dict(image_emb=image_emb, text_emb=text_emb, positive=positive, loss_scale=loss_scale)


temper = 32.0
offset = -2.0
epsilon = 1e-06

def normalize(emb):
    wide = emb.astype(jnp.float32)
    inv_norm = lax.rsqrt(lax.optimization_barrier(jnp.sum(wide * wide, axis=1, keepdims=True)) + epsilon)
    return (wide * inv_norm, inv_norm)

def finish(unit_vec, inv_norm, d_unit):
    row_dots = lax.optimization_barrier(jnp.sum(unit_vec * d_unit, axis=1, keepdims=True))
    return ((d_unit - unit_vec * row_dots) * inv_norm).astype(jnp.bfloat16)

def reference(image_emb, text_emb, positive, loss_scale):
    unit_img, inv_img = normalize(image_emb)
    unit_txt, inv_txt = normalize(text_emb)
    img_half = unit_img.astype(jnp.bfloat16)
    txt_half = unit_txt.astype(jnp.bfloat16)
    weight_scale = loss_scale * temper / IMAGES
    text_ids = jnp.arange(TEXTS, dtype=jnp.int32)
    img_blocks = img_half.reshape(IMAGES // IMG_DEV, IMG_DEV, D)
    pos_blocks = positive.reshape(IMAGES // IMG_DEV, IMG_DEV)

    def one_block(text_acc, inputs):
        block_half, block_pos = inputs
        logits = temper * lax.dot_general(block_half, txt_half, (((1,), (1,)), ((), ())), preferred_element_type=jnp.float32) + offset
        is_positive = (block_pos[:, None] == text_ids[None, :]).astype(jnp.float32)
        grad_tile = (weight_scale * (jax.nn.sigmoid(logits) - is_positive)).astype(jnp.bfloat16)
        d_block = jnp.dot(grad_tile, txt_half, preferred_element_type=jnp.float32)
        text_acc = text_acc + lax.dot_general(grad_tile, block_half, (((0,), (0,)), ((), ())), preferred_element_type=jnp.float32)
        return (text_acc, d_block)
    start_acc = jnp.zeros((TEXTS, D), jnp.float32)
    d_unit_txt, d_blocks = lax.scan(one_block, start_acc, (img_blocks, pos_blocks))
    d_unit_img = d_blocks.reshape(IMAGES, D)
    return (finish(unit_img, inv_img, d_unit_img), finish(unit_txt, inv_txt, d_unit_txt))
```

```python
import functools

import jax
import jax.numpy as jnp
import numpy as np
from jax import lax
from jax.experimental import pallas as pl
from jax.experimental.pallas import tpu as pltpu
from jax.sharding import PartitionSpec as P

temper = 32.0
offset = -2.0
epsilon = 1e-06
F32 = jnp.float32
BF16 = jnp.bfloat16
AXES = ("img", "txt")
NX, NY, NZ = 4, 4, 8
VMEM_LIMIT = 40 * 1024 * 1024


def line(z, y, x, c):
    return ((z * 2 + y // 2) * 2 + y % 2) * (NX * 2) + x * 2 + c


def make_perm(move):
    pairs = []
    for z in range(NZ):
        for y in range(NY):
            for x in range(NX):
                for c in range(2):
                    tz, ty, tx, tc = move(z, y, x, c, 1 - 2 * c)
                    pairs.append((line(z, y, x, c), line(tz % NZ, ty % NY, tx % NX, tc)))
    return pairs


CORE = make_perm(lambda z, y, x, c, s: (z, y, x, 1 - c))
Z_ON = make_perm(lambda z, y, x, c, s: (z + s, y, x, c))
X_ON = make_perm(lambda z, y, x, c, s: (z, y, x + s, c))
X_BACK = make_perm(lambda z, y, x, c, s: (z, y, x - s, c))
X_TWO = make_perm(lambda z, y, x, c, s: (z, y, x + 2, c))
Y_ON = make_perm(lambda z, y, x, c, s: (z, y + s, x, c))
Y_BACK = make_perm(lambda z, y, x, c, s: (z, y - s, x, c))
Y_TWO = make_perm(lambda z, y, x, c, s: (z, y + 2, x, c))


def send(v, perm):
    return lax.ppermute(v, AXES, perm)


def wide_inv(raw):
    wide = raw.astype(F32)
    return wide, lax.rsqrt(jnp.sum(wide * wide, axis=1, keepdims=True) + epsilon)


def project(raw, d):
    wide, inv = wide_inv(raw)
    unit = wide * inv
    dots = jnp.sum(unit * d, axis=1, keepdims=True)
    return ((d - unit * dots) * inv).astype(BF16)


def norm_kernel(*refs):
    pieces, out = refs[:-1], refs[-1]
    row = 0
    for p in pieces:
        n = p.shape[0]
        wide, inv = wide_inv(p[...])
        out[row : row + n, :] = (wide * inv).astype(BF16)
        row += n


def text_kernel(base_ref, scale_ref, pos_ref, xh_ref, *refs):
    pieces = refs[:-5]
    g_ref, yh_ref, out_ref, d_ref, id_ref = refs[-5:]
    rows = yh_ref.shape[0]
    row = 0
    for p in pieces:
        n = p.shape[0]
        wide, inv = wide_inv(p[...])
        yh_ref[row : row + n, :] = (wide * inv).astype(BF16)
        row += n
    for k in range(rows // 64):
        id_ref[k * 64 : (k + 1) * 64, :] = base_ref[k] + lax.broadcasted_iota(
            jnp.int32, (64, 128), 0
        )
    scale = scale_ref[0]
    images = xh_ref.shape[0]
    for n in range(0, images, 256):
        logits = (
            temper
            * lax.dot_general(
                yh_ref[...],
                xh_ref[n : n + 256, :],
                (((1,), (1,)), ((), ())),
                preferred_element_type=F32,
            )
            + offset
        )
        same = pos_ref[:, n : n + 256] == jnp.concatenate([id_ref[...]] * 2, axis=1)
        g_ref[:, n : n + 256] = (
            scale * (jax.nn.sigmoid(logits) - same.astype(F32))
        ).astype(BF16)
    width = xh_ref.shape[1]
    for n in range(0, width, 384):
        d_ref[:, n : n + 384] = jnp.dot(
            g_ref[...], xh_ref[:, n : n + 384], preferred_element_type=F32
        )
    row = 0
    for p in pieces:
        n = p.shape[0]
        out_ref[row : row + n, :] = project(p[...], d_ref[row : row + n, :])
        row += n


def image_kernel(ga_ref, gb_ref, ya_ref, yb_ref, *refs):
    count = (len(refs) - 1) // 2
    pieces, outs, d_ref = refs[:count], refs[count:-1], refs[-1]
    width = ya_ref.shape[1]
    for half in range(2):
        cols = slice(half * 512, half * 512 + 512)
        for n in range(0, width, 384):
            d_ref[:, n : n + 384] = lax.dot_general(
                ga_ref[:, cols],
                ya_ref[:, n : n + 384],
                (((0,), (0,)), ((), ())),
                preferred_element_type=F32,
            ) + lax.dot_general(
                gb_ref[:, cols],
                yb_ref[:, n : n + 384],
                (((0,), (0,)), ((), ())),
                preferred_element_type=F32,
            )
        for k in range(4):
            j = half * 4 + k
            outs[j][...] = project(pieces[j][...], d_ref[k * 128 : k * 128 + 128, :])


VM = pl.BlockSpec(memory_space=pltpu.VMEM)
SM = pl.BlockSpec(memory_space=pltpu.SMEM)
PARAMS = pltpu.CompilerParams(vmem_limit_bytes=VMEM_LIMIT)


def sds(shape, dtype):
    return jax.ShapeDtypeStruct(shape, dtype)


def normalize_all(pieces):
    rows = sum(p.shape[0] for p in pieces)
    width = pieces[0].shape[1]
    return pl.pallas_call(
        norm_kernel,
        out_shape=sds((rows, width), BF16),
        in_specs=[VM] * len(pieces),
        out_specs=VM,
        compiler_params=PARAMS,
        cost_estimate=pl.CostEstimate(flops=4 * rows * width, bytes_accessed=4 * rows * width, transcendentals=0),
        name="normalize_images",
    )(*pieces)


def text_part(bases, scale, pos, xh, pieces, name):
    rows = sum(p.shape[0] for p in pieces)
    images, width = xh.shape
    return pl.pallas_call(
        text_kernel,
        out_shape=(sds((rows, images), BF16), sds((rows, width), BF16), sds((rows, width), BF16)),
        in_specs=[SM, SM, VM, VM] + [VM] * len(pieces),
        out_specs=(VM, VM, VM),
        scratch_shapes=[pltpu.VMEM((rows, width), F32), pltpu.VMEM((rows, 128), jnp.int32)],
        compiler_params=PARAMS,
        cost_estimate=pl.CostEstimate(
            flops=4 * rows * images * width, bytes_accessed=8 * rows * width, transcendentals=rows * images
        ),
        name=name,
    )(bases, scale, pos, xh, *pieces)


def image_part(ga, gb, ya, yb, pieces):
    width = ya.shape[1]
    return pl.pallas_call(
        image_kernel,
        out_shape=tuple(sds(p.shape, BF16) for p in pieces),
        in_specs=[VM] * (4 + len(pieces)),
        out_specs=tuple([VM] * len(pieces)),
        scratch_shapes=[pltpu.VMEM((512, width), F32)],
        compiler_params=PARAMS,
        cost_estimate=pl.CostEstimate(
            flops=2 * 1024 * 1024 * width, bytes_accessed=8 * 1024 * width, transcendentals=0
        ),
        name="image_sums",
    )(ga, gb, ya, yb, *pieces)


def add(*terms):
    total = terms[0].astype(F32)
    for t in terms[1:]:
        total = total + t.astype(F32)
    return total


def four(own, on, back, two):
    return own, send(own, on), send(own, back), send(own, two)


def four_forward(own, on, back):
    first = send(own, on)
    return own, first, send(own, back), send(first, on)


def ring_sum(parts, on, back):
    at0, at_back, at_on, at_two = parts
    far = send(at_two.astype(BF16), on)
    near = send(add(at_on, far).astype(BF16), on)
    other = send(at_back.astype(BF16), back)
    return add(at0, near, other)


def relative(arr, at, s, axis):
    rolled = jnp.roll(arr, -at, axis=axis)
    p = [lax.slice_in_dim(rolled, k, k + 1, axis=axis) for k in range(4)]
    up = jnp.concatenate([p[0], p[3], p[1], p[2]], axis=axis)
    down = jnp.concatenate([p[0], p[1], p[3], p[2]], axis=axis)
    return jnp.where(s > 0, up, down)


def local(image_emb, text_emb, positive, loss_scale):
    i, t = lax.axis_index("img"), lax.axis_index("txt")
    z, yh = i // 2, i % 2
    yl, x, c = t // 8, (t // 2) % 4, t % 2
    y = yh * 2 + yl
    s = 1 - 2 * c
    half = image_emb.shape[0] // 2

    other = send(text_emb, CORE)
    chip = jnp.concatenate([text_emb, other], axis=0)
    img_a, img_b = image_emb[:half], image_emb[half:]
    r1 = send(chip, Z_ON)
    a4 = jnp.concatenate(four(img_a, X_ON, X_BACK, X_TWO), axis=0)
    b4 = jnp.concatenate(four(img_b, Y_ON, Y_BACK, Y_TWO), axis=0)
    r2 = send(r1, Z_ON)
    a_all = four_forward(a4, Y_ON, Y_BACK)
    b_all = four_forward(b4, X_ON, X_BACK)
    r3 = send(r2, Z_ON)
    r4 = send(r3[:64], Z_ON)
    q1, q2, q3, q4 = (send(r, CORE) for r in (r1, r2, r3, r4))

    mine = lax.dynamic_index_in_dim(positive.reshape(2, 4, 2, 64), c, axis=2, keepdims=False)
    across = send(mine, Y_TWO)
    low = jnp.where(yh == 0, mine, across)
    high = jnp.where(yh == 0, across, mine)
    grid = jnp.concatenate([low, high], axis=0)
    grid = relative(relative(grid, y, s, 0), x, s, 1)
    pos = jnp.concatenate(
        [grid[:, :, :half].reshape(-1), jnp.swapaxes(grid[:, :, half:], 0, 1).reshape(-1)]
    ).reshape(1, -1)

    def text_base(zz, cc):
        return ((((yl * 4 + x) * 2 + cc) * 8 + zz % 8) * 2 + yh) * 64

    d = 1 - c
    keep_at = [(z + s, d), (z + s, c), (z + 2 * s, d), (z + 2 * s, c), (z + 3 * s, d), (z + 3 * s, c), (z + 4, d), (z, c)]
    give_at = [(z - s, c), (z - s, d), (z - 2 * s, c), (z - 2 * s, d), (z - 3 * s, c), (z - 3 * s, d), (z + 4, c), (z, d)]
    keep_base = jnp.stack([text_base(*at) for at in keep_at]).astype(jnp.int32)
    give_base = jnp.stack([text_base(*at) for at in give_at]).astype(jnp.int32)
    scale = (loss_scale * (temper / 16384.0)).reshape(1)

    pieces = a_all + b_all
    xh = normalize_all(pieces)
    g_give, y_give, d_give = text_part(give_base, scale, pos, xh, (r1, r2, r3, r4, other), "give_texts")
    swapped = send(d_give, CORE)
    g_keep, y_keep, d_keep = text_part(keep_base, scale, pos, xh, (q1, q2, q3, q4, text_emb), "keep_texts")

    total = add(d_keep, swapped)
    far = send(total[384:448].astype(BF16), Z_ON)
    t3 = jnp.concatenate([add(total[256:320], far), total[320:384]], axis=0)
    got = send(t3.astype(BF16), Z_ON)
    got = send(add(total[128:256], got).astype(BF16), Z_ON)
    got = send(add(total[0:128], got).astype(BF16), Z_ON)
    last = send(got[:64], CORE)
    grad_text = add(total[448:512], got[64:], last).astype(BF16)

    parts = image_part(g_give, g_keep, y_give, y_keep, pieces)
    sum_a = ring_sum(parts[:4], Y_ON, Y_BACK)
    sum_b = ring_sum(parts[4:], X_ON, X_BACK)
    out_a = ring_sum([sum_a[k * half : (k + 1) * half] for k in range(4)], X_ON, X_BACK)
    out_b = ring_sum([sum_b[k * half : (k + 1) * half] for k in range(4)], Y_ON, Y_BACK)
    grad_image = jnp.concatenate([out_a, out_b], axis=0).astype(BF16)
    return grad_image, grad_text


def solution(mesh):
    in_specs = (P(("img", "txt"), None), P(("txt", "img"), None), P("img"), P())
    out_specs = (P(("img", "txt"), None), P(("txt", "img"), None))
    return jax.shard_map(local, mesh=mesh, in_specs=in_specs, out_specs=out_specs, check_vma=False)
```

```python
import functools

import jax
import jax.numpy as jnp
import numpy as np
from jax import lax
from jax.experimental import pallas as pl
from jax.experimental.pallas import tpu as pltpu
from jax.sharding import PartitionSpec as P

temper = 32.0
offset = -2.0
epsilon = 1e-06
F32 = jnp.float32
BF16 = jnp.bfloat16
AXES = ("img", "txt")
NX, NY, NZ = 4, 4, 8
VMEM_LIMIT = 40 * 1024 * 1024


def line(z, y, x, c):
    return ((z * 2 + y // 2) * 2 + y % 2) * (NX * 2) + x * 2 + c


def make_perm(move):
    pairs = []
    for z in range(NZ):
        for y in range(NY):
            for x in range(NX):
                for c in range(2):
                    tz, ty, tx, tc = move(z, y, x, c, 1 - 2 * c)
                    pairs.append((line(z, y, x, c), line(tz % NZ, ty % NY, tx % NX, tc)))
    return pairs


CORE = make_perm(lambda z, y, x, c, s: (z, y, x, 1 - c))
Z_ONE = make_perm(lambda z, y, x, c, s: (z + s, y, x, c))
Z_TWO = make_perm(lambda z, y, x, c, s: (z + 2 * s, y, x, c))


def shift_perm(first, by):
    return make_perm(
        lambda z, y, x, c, s: (z, y, x + by, c) if (c == 0) == first else (z, y + by, x, c)
    )


A_ON, A_BACK, A_TWO = (shift_perm(True, by) for by in (1, -1, 2))
B_ON, B_BACK, B_TWO = (shift_perm(False, by) for by in (1, -1, 2))
Y_TWO = make_perm(lambda z, y, x, c, s: (z, y + 2, x, c))


def send(v, perm):
    return lax.ppermute(v, AXES, perm)


def wide_inv(raw):
    wide = raw.astype(F32)
    return wide, lax.rsqrt(jnp.sum(wide * wide, axis=1, keepdims=True) + epsilon)


def project(raw, d):
    wide, inv = wide_inv(raw)
    unit = wide * inv
    dots = jnp.sum(unit * d, axis=1, keepdims=True)
    return ((d - unit * dots) * inv).astype(BF16)


def norm_kernel(*refs):
    pieces, out = refs[:-1], refs[-1]
    row = 0
    for p in pieces:
        n = p.shape[0]
        wide, inv = wide_inv(p[...])
        out[row : row + n, :] = (wide * inv).astype(BF16)
        row += n


def join_kernel(*refs):
    row = 0
    for p in refs[:-1]:
        n = p.shape[0]
        refs[-1][row : row + n, :] = p[...]
        row += n


def tile_body(base_ref, scale_ref, pos_ref, raw_ref, yh_ref, g_ref, xh_ref):
    wide, inv = wide_inv(raw_ref[...])
    xh_ref[...] = (wide * inv).astype(BF16)
    scale = scale_ref[0]
    images = raw_ref.shape[0]
    texts = yh_ref.shape[0]
    step = 512
    for n in range(0, texts, step):
        logits = (
            temper
            * lax.dot_general(
                yh_ref[n : n + step, :],
                xh_ref[...],
                (((1,), (1,)), ((), ())),
                preferred_element_type=F32,
            )
            + offset
        )
        row = lax.broadcasted_iota(jnp.int32, (64, images), 0)
        ids = jnp.concatenate([row + base_ref[(n + m) // 64] for m in range(0, step, 64)], axis=0)
        same = (pos_ref[...] == ids).astype(F32)
        g_ref[n : n + step, :] = (scale * (jax.nn.sigmoid(logits) - same)).astype(BF16)


def image_body(raw_ref, yh_ref, g_ref, out_ref, d_ref):
    width = yh_ref.shape[1]
    for n in range(0, width, 384):
        d_ref[:, n : n + 384] = lax.dot_general(
            g_ref[...],
            yh_ref[:, n : n + 384],
            (((0,), (0,)), ((), ())),
            preferred_element_type=F32,
        )
    out_ref[...] = project(raw_ref[...], d_ref[...])


def tile_kernel(base_ref, scale_ref, pos_ref, raw_ref, yh_ref, g_ref, xh_ref):
    tile_body(base_ref, scale_ref, pos_ref, raw_ref, yh_ref, g_ref, xh_ref)


def image_kernel(raw_ref, yh_ref, g_ref, out_ref, d_ref):
    image_body(raw_ref, yh_ref, g_ref, out_ref, d_ref)


def both_kernel(base_ref, scale_ref, pos_ref, raw_ref, yh_ref, g_ref, xh_ref, out_ref, d_ref):
    tile_body(base_ref, scale_ref, pos_ref, raw_ref, yh_ref, g_ref, xh_ref)
    image_body(raw_ref, yh_ref, g_ref, out_ref, d_ref)


def text_kernel(first, *refs):
    gs, xs, pieces = refs[:4], refs[4:8], refs[8:-2]
    out_ref, d_ref = refs[-2:]
    rows, width = out_ref.shape
    for n in range(0, width, 384):
        total = None
        for g, x in zip(gs, xs):
            part = jnp.dot(
                g[first : first + rows, :], x[:, n : n + 384], preferred_element_type=F32
            )
            total = part if total is None else total + part
        d_ref[:, n : n + 384] = total
    row = 0
    for p in pieces:
        n = p.shape[0]
        out_ref[row : row + n, :] = project(p[...], d_ref[row : row + n, :])
        row += n


VM = pl.BlockSpec(memory_space=pltpu.VMEM)
SM = pl.BlockSpec(memory_space=pltpu.SMEM)
PARAMS = pltpu.CompilerParams(vmem_limit_bytes=VMEM_LIMIT)


def sds(shape, dtype):
    return jax.ShapeDtypeStruct(shape, dtype)


def cost(flops, nbytes, trans=0):
    return pl.CostEstimate(flops=flops, bytes_accessed=nbytes, transcendentals=trans)


def join(*pieces):
    rows = sum(p.shape[0] for p in pieces)
    width = pieces[0].shape[1]
    return pl.pallas_call(
        join_kernel,
        out_shape=sds((rows, width), BF16),
        in_specs=[VM] * len(pieces),
        out_specs=VM,
        compiler_params=PARAMS,
        cost_estimate=cost(0, 4 * rows * width),
        name="join",
    )(*pieces)


def normalize_all(pieces):
    rows = sum(p.shape[0] for p in pieces)
    width = pieces[0].shape[1]
    return pl.pallas_call(
        norm_kernel,
        out_shape=sds((rows, width), BF16),
        in_specs=[VM] * len(pieces),
        out_specs=VM,
        compiler_params=PARAMS,
        cost_estimate=cost(4 * rows * width, 4 * rows * width),
        name="normalize_texts",
    )(*pieces)


def tile(bases, scale, pos, raw, yh, with_image):
    images, width = raw.shape
    texts = yh.shape[0]
    outs = [sds((texts, images), BF16), sds((images, width), BF16)]
    scratch = []
    if with_image:
        outs.append(sds((images, width), BF16))
        scratch.append(pltpu.VMEM((images, width), F32))
    return pl.pallas_call(
        both_kernel if with_image else tile_kernel,
        out_shape=tuple(outs),
        in_specs=[SM, SM, VM, VM, VM],
        out_specs=tuple([VM] * len(outs)),
        scratch_shapes=scratch,
        compiler_params=PARAMS,
        cost_estimate=cost(
            (4 if with_image else 2) * texts * images * width, 4 * (texts + images) * width, texts * images
        ),
        name="tile_and_image" if with_image else "tile",
    )(bases, scale, pos, raw, yh)


def image_sum(raw, yh, g):
    images, width = raw.shape
    return pl.pallas_call(
        image_kernel,
        out_shape=sds((images, width), BF16),
        in_specs=[VM] * 3,
        out_specs=VM,
        scratch_shapes=[pltpu.VMEM((images, width), F32)],
        compiler_params=PARAMS,
        cost_estimate=cost(2 * yh.shape[0] * images * width, 4 * images * width),
        name="image_sum",
    )(raw, yh, g)


def text_sum(first, gs, xs, pieces, name):
    rows = sum(p.shape[0] for p in pieces)
    width = pieces[0].shape[1]
    return pl.pallas_call(
        functools.partial(text_kernel, first),
        out_shape=sds((rows, width), BF16),
        in_specs=[VM] * (8 + len(pieces)),
        out_specs=VM,
        scratch_shapes=[pltpu.VMEM((rows, width), F32)],
        compiler_params=PARAMS,
        cost_estimate=cost(2 * rows * 1024 * width, 8 * rows * width),
        name=name,
    )(*gs, *xs, *pieces)


def add(*terms):
    total = terms[0].astype(F32)
    for t in terms[1:]:
        total = total + t.astype(F32)
    return total


def relative(arr, at, axis):
    rolled = jnp.roll(arr, -at, axis=axis)
    p = [lax.slice_in_dim(rolled, k, k + 1, axis=axis) for k in range(4)]
    return jnp.concatenate([p[0], p[3], p[1], p[2]], axis=axis)


def local(image_emb, text_emb, positive, loss_scale):
    i, t = lax.axis_index("img"), lax.axis_index("txt")
    z, yh = i // 2, i % 2
    yl, x, c = t // 8, (t // 2) % 4, t % 2
    y = yh * 2 + yl
    s = 1 - 2 * c
    d = 1 - c

    other = send(text_emb, CORE)
    chip = join(text_emb, other)

    row = join(image_emb, send(image_emb, A_ON), send(image_emb, A_BACK), send(image_emb, A_TWO))
    quarters = [row, send(row, B_ON), send(row, B_BACK), send(row, B_TWO)]

    near = send(chip, Z_ONE)
    second = send(chip, Z_TWO)
    third = send(second, Z_ONE)
    fourth = send(second[:64], Z_TWO)
    cross = [send(join(near, second), CORE), send(join(third, fourth), CORE)]
    give_pieces = [near, second, third, fourth, other]
    keep_pieces = cross + [text_emb]

    mine = lax.dynamic_index_in_dim(positive.reshape(2, 4, 2, 64), c, axis=2, keepdims=False)
    across = send(mine, Y_TWO)
    low = jnp.where(yh == 0, mine, across)
    high = jnp.where(yh == 0, across, mine)
    grid = jnp.concatenate([low, high], axis=0)
    grid = relative(relative(grid, y, 0), x, 1)
    grid = jnp.where(c == 0, grid, jnp.swapaxes(grid, 0, 1)).reshape(4, 1, 256)

    def text_base(zz, cc):
        return ((((yl * 4 + x) * 2 + cc) * 8 + zz % 8) * 2 + yh) * 64

    give_at = [(z - k * s, cc) for k in (1, 2, 3) for cc in (c, d)] + [(z + 4, c), (z, d)]
    keep_at = [(z + k * s, cc) for k in (1, 2, 3) for cc in (d, c)] + [(z + 4, d), (z, c)]
    bases = jnp.stack([text_base(*at) for at in give_at + keep_at]).astype(jnp.int32)
    scale = (loss_scale * (temper / 16384.0)).reshape(1)

    yh_all = normalize_all(give_pieces + keep_pieces)
    gs, xs, es = [], [], []
    for k in range(3):
        g, xn, e = tile(bases, scale, grid[k], quarters[k], yh_all, True)
        gs.append(g)
        xs.append(xn)
        es.append(e)
    g, xn = tile(bases, scale, grid[3], quarters[3], yh_all, False)
    gs.append(g)
    xs.append(xn)

    d_give = text_sum(0, gs, xs, give_pieces, "give_texts")
    swapped = send(d_give, CORE)
    d_keep = text_sum(512, gs, xs, keep_pieces, "keep_texts")
    es.append(image_sum(quarters[3], yh_all, gs[3]))
    total = add(d_keep, swapped)
    far = send(total[256:448].astype(BF16), Z_TWO)
    half = add(total[0:192], far).astype(BF16)
    w2 = send(jnp.concatenate([half[128:192], total[192:256].astype(BF16)], axis=0), Z_TWO)
    w1 = send(half[0:128], Z_ONE)
    to_other = add(w1[:64], w2[:64]).astype(BF16)
    last = send(to_other, CORE)
    grad_text = add(total[448:512], w1[64:], w2[64:], last).astype(BF16)

    back = [send(es[1], B_BACK), send(es[2], B_ON), send(es[3], B_TWO)]
    row_sum = add(es[0], *back)
    row_half = row_sum.astype(BF16)
    home = [send(row_half[64:128], A_BACK), send(row_half[128:192], A_ON), send(row_half[192:256], A_TWO)]
    grad_image = add(row_sum[:64], *home).astype(BF16)
    return grad_image, grad_text


def solution(mesh):
    in_specs = (P(("img", "txt"), None), P(("txt", "img"), None), P("img"), P())
    out_specs = (P(("img", "txt"), None), P(("txt", "img"), None))
    return jax.shard_map(local, mesh=mesh, in_specs=in_specs, out_specs=out_specs, check_vma=False)
```

```python
import functools

import jax
import jax.numpy as jnp
import numpy as np
from jax import lax
from jax.experimental import pallas as pl
from jax.experimental.pallas import tpu as pltpu
from jax.sharding import PartitionSpec as P

temper = 32.0
offset = -2.0
epsilon = 1e-06
F32 = jnp.float32
BF16 = jnp.bfloat16
AXES = ("img", "txt")
NX, NY, NZ = 4, 4, 8
VMEM_LIMIT = 16 * 1024 * 1024


def line(z, y, x, c):
    return ((z * 2 + y // 2) * 2 + y % 2) * (NX * 2) + x * 2 + c


def make_perm(move):
    pairs = []
    for z in range(NZ):
        for y in range(NY):
            for x in range(NX):
                for c in range(2):
                    tz, ty, tx, tc = move(z, y, x, c, 1 - 2 * c)
                    pairs.append((line(z, y, x, c), line(tz % NZ, ty % NY, tx % NX, tc)))
    return pairs


CORE = make_perm(lambda z, y, x, c, s: (z, y, x, 1 - c))
Z_ONE = make_perm(lambda z, y, x, c, s: (z + s, y, x, c))
Z_TWO = make_perm(lambda z, y, x, c, s: (z + 2 * s, y, x, c))


def shift_perm(first, by):
    return make_perm(
        lambda z, y, x, c, s: (z, y, x + by, c) if (c == 0) == first else (z, y + by, x, c)
    )


A_ON, A_BACK, A_TWO = (shift_perm(True, by) for by in (1, -1, 2))
B_ON, B_BACK, B_TWO = (shift_perm(False, by) for by in (1, -1, 2))
Y_TWO = make_perm(lambda z, y, x, c, s: (z, y + 2, x, c))


def send(v, perm):
    return lax.ppermute(v, AXES, perm)


def wide_inv(raw):
    wide = raw.astype(F32)
    return wide, lax.rsqrt(jnp.sum(wide * wide, axis=1, keepdims=True) + epsilon)


def project(raw, d):
    wide, inv = wide_inv(raw)
    unit = wide * inv
    dots = jnp.sum(unit * d, axis=1, keepdims=True)
    return ((d - unit * dots) * inv).astype(BF16)


def join_kernel(*refs):
    row = 0
    for p in refs[:-1]:
        n = p.shape[0]
        refs[-1][row : row + n, :] = p[...]
        row += n


def norm_kernel(*refs):
    pieces, out = refs[:-1], refs[-1]
    row = 0
    for p in pieces:
        n = p.shape[0]
        wide, inv = wide_inv(p[...])
        out[row : row + n, :] = (wide * inv).astype(BF16)
        row += n


def setup_kernel(tab_ref, scale_ref, own_ref, across_ref, pos_ref, near_ref, far_ref, weight_ref):
    core = tab_ref[48]
    for k in range(4):
        parts = []
        for j in range(4 * k, 4 * k + 4):
            at = pl.ds(tab_ref[16 + j], 1)
            both = jnp.where(tab_ref[32 + j] == 1, own_ref[at, :], across_ref[at, :])
            parts.append(jnp.where(core == 0, both[:, :64], both[:, 64:]))
        pos_ref[k : k + 1, :] = jnp.concatenate(parts, axis=1)
    row = lax.broadcasted_iota(jnp.int32, (64, 128), 0)
    for b in range(10):
        near_ref[b * 64 : b * 64 + 64, :] = row + tab_ref[b]
    for b in range(6):
        far_ref[b * 64 : b * 64 + 64, :] = row + tab_ref[10 + b]
    weight_ref[...] = jnp.full(weight_ref.shape, scale_ref[0], F32)


def tile_body(quarter, weight_ref, pos_ref, ids_ref, xh_ref, yh_ref, g_ref):
    images = xh_ref.shape[0]
    weight = weight_ref[0:1, :]
    pos = pos_ref[quarter : quarter + 1, :]
    logits = (
        temper
        * lax.dot_general(
            yh_ref[...], xh_ref[...], (((1,), (1,)), ((), ())), preferred_element_type=F32
        )
        + offset
    )
    half = jax.nn.sigmoid(logits)
    for n in range(0, images, 128):
        cols = slice(n, n + 128)
        same = (pos[:, cols] == ids_ref[...]).astype(F32)
        g_ref[:, cols] = (weight * (half[:, cols] - same)).astype(BF16)


def near_kernel(quarter, weight_ref, pos_ref, ids_ref, raw_ref, yh_ref, g_ref, xh_ref, part_ref):
    wide, inv = wide_inv(raw_ref[...])
    xh_ref[...] = (wide * inv).astype(BF16)
    tile_body(quarter, weight_ref, pos_ref, ids_ref, xh_ref, yh_ref, g_ref)
    width = yh_ref.shape[1]
    for n in range(0, width, 384):
        part_ref[:, n : n + 384] = lax.dot_general(
            g_ref[...], yh_ref[:, n : n + 384], (((0,), (0,)), ((), ())), preferred_element_type=F32
        )


def far_kernel(quarter, weight_ref, pos_ref, ids_ref, xh_ref, yh_ref, g_ref):
    tile_body(quarter, weight_ref, pos_ref, ids_ref, xh_ref, yh_ref, g_ref)


def image_kernel(raw_ref, yh_ref, part_ref, g_ref, out_ref, d_ref):
    width = yh_ref.shape[1]
    for n in range(0, width, 384):
        d_ref[:, n : n + 384] = part_ref[:, n : n + 384] + lax.dot_general(
            g_ref[...], yh_ref[:, n : n + 384], (((0,), (0,)), ((), ())), preferred_element_type=F32
        )
    out_ref[...] = project(raw_ref[...], d_ref[...])


def text_kernel(first, *refs):
    gs, xs, pieces = refs[:4], refs[4:8], refs[8:-2]
    out_ref, d_ref = refs[-2:]
    rows, width = out_ref.shape
    for n in range(0, width, 384):
        total = None
        for g, x in zip(gs, xs):
            part = jnp.dot(
                g[first : first + rows, :], x[:, n : n + 384], preferred_element_type=F32
            )
            total = part if total is None else total + part
        d_ref[:, n : n + 384] = total
    row = 0
    for p in pieces:
        n = p.shape[0]
        out_ref[row : row + n, :] = project(p[...], d_ref[row : row + n, :])
        row += n


VM = pl.BlockSpec(memory_space=pltpu.VMEM)
SM = pl.BlockSpec(memory_space=pltpu.SMEM)
PARAMS = pltpu.CompilerParams(vmem_limit_bytes=VMEM_LIMIT)


def sds(shape, dtype):
    return jax.ShapeDtypeStruct(shape, dtype)


WEIGHT = 0.1


def fast(*arrays):
    return [pltpu.with_memory_space_constraint(a, pltpu.VMEM) for a in arrays]


def cost(us):
    return pl.CostEstimate(flops=int(us * WEIGHT * 1.15e9), bytes_accessed=1, transcendentals=0)


def join(*pieces, weight=0.3):
    rows = sum(p.shape[0] for p in pieces)
    width = pieces[0].shape[1]
    return pl.pallas_call(
        join_kernel,
        out_shape=sds((rows, width), BF16),
        in_specs=[VM] * len(pieces),
        out_specs=VM,
        compiler_params=PARAMS,
        cost_estimate=cost(weight),
        name="join",
    )(*fast(*pieces))


def copy(piece):
    return join(piece)


def normalize_all(*pieces):
    rows = sum(p.shape[0] for p in pieces)
    width = pieces[0].shape[1]
    return pl.pallas_call(
        norm_kernel,
        out_shape=sds((rows, width), BF16),
        in_specs=[VM] * len(pieces),
        out_specs=VM,
        compiler_params=PARAMS,
        cost_estimate=cost(0.4),
        name="normalize_texts",
    )(*fast(*pieces))


def setup(tab, scale, own, across):
    return pl.pallas_call(
        setup_kernel,
        out_shape=(
            sds((4, 256), jnp.int32),
            sds((640, 128), jnp.int32),
            sds((384, 128), jnp.int32),
            sds((8, 128), F32),
        ),
        in_specs=[SM, SM, VM, VM],
        out_specs=(VM, VM, VM, VM),
        compiler_params=PARAMS,
        cost_estimate=cost(1),
        name="setup",
    )(tab, scale, own, across)


def near_part(quarter, weight, pos, ids, raw, yh):
    images, width = raw.shape
    texts = yh.shape[0]
    return pl.pallas_call(
        functools.partial(near_kernel, quarter),
        out_shape=(sds((texts, images), BF16), sds((images, width), BF16), sds((images, width), F32)),
        in_specs=[VM] * 5,
        out_specs=(VM, VM, VM),
        compiler_params=PARAMS,
        cost_estimate=cost(2.15),
        name="near_tile",
    )(*fast(weight, pos, ids, raw, yh))


def far_part(quarter, weight, pos, ids, xh, yh):
    images, width = xh.shape
    texts = yh.shape[0]
    return pl.pallas_call(
        functools.partial(far_kernel, quarter),
        out_shape=sds((texts, images), BF16),
        in_specs=[VM] * 5,
        out_specs=VM,
        compiler_params=PARAMS,
        cost_estimate=cost(1.13),
        name="far_tile",
    )(*fast(weight, pos, ids, xh, yh))


def image_sum(raw, yh, part, g):
    images, width = raw.shape
    return pl.pallas_call(
        image_kernel,
        out_shape=sds((images, width), BF16),
        in_specs=[VM] * 4,
        out_specs=VM,
        scratch_shapes=[pltpu.VMEM((images, width), F32)],
        compiler_params=PARAMS,
        cost_estimate=cost(0.8),
        name="image_sum",
    )(*fast(raw, yh, part, g))


def text_sum(first, gs, xs, pieces, name):
    rows = sum(p.shape[0] for p in pieces)
    width = pieces[0].shape[1]
    return pl.pallas_call(
        functools.partial(text_kernel, first),
        out_shape=sds((rows, width), BF16),
        in_specs=[VM] * (8 + len(pieces)),
        out_specs=VM,
        scratch_shapes=[pltpu.VMEM((rows, width), F32)],
        compiler_params=PARAMS,
        cost_estimate=cost(rows / 230),
        name=name,
    )(*fast(*gs, *xs, *pieces))


def add(*terms):
    total = terms[0].astype(F32)
    for t in terms[1:]:
        total = total + t.astype(F32)
    return total


def local(image_emb, text_emb, positive, loss_scale):
    i, t = lax.axis_index("img"), lax.axis_index("txt")
    z, yh = i // 2, i % 2
    yl, x, c = t // 8, (t // 2) % 4, t % 2
    y = yh * 2 + yl
    s = 1 - 2 * c
    d = 1 - c

    other = send(text_emb, CORE)
    own_images = copy(image_emb)
    own_pairs = positive.reshape(8, 128)
    across_pairs = send(own_pairs, Y_TWO)

    def text_base(zz, cc):
        return ((((yl * 4 + x) * 2 + cc) * 8 + zz % 8) * 2 + yh) * 64

    at = [(z - s, c), (z - s, d), (z - 2 * s, c), (z - 2 * s, d), (z, d)]
    at += [(z + s, d), (z + s, c), (z + 2 * s, d), (z + 2 * s, c), (z, c)]
    at += [(z - 3 * s, c), (z - 3 * s, d), (z + 4, c)]
    at += [(z + 3 * s, d), (z + 3 * s, c), (z + 4, d)]
    table = [text_base(*p) for p in at]
    rows, mine = [], []
    for b in (0, -1, 1, 2):
        for a in (0, -1, 1, 2):
            yy = (y + jnp.where(c == 0, b, a)) % 4
            xx = (x + jnp.where(c == 0, a, b)) % 4
            rows.append(yy % 2 * 4 + xx)
            mine.append((yy // 2 == yh).astype(jnp.int32))
    tab = jnp.stack([v.astype(jnp.int32) for v in table + rows + mine + [c]])
    scale = (loss_scale * (temper / 16384.0)).reshape(1)
    pos, near_ids, far_ids, weight = setup(tab, scale, own_pairs, across_pairs)

    own_images, pos = lax.optimization_barrier((own_images, pos))
    row = join(own_images, send(image_emb, A_ON), send(image_emb, A_BACK), send(image_emb, A_TWO))
    quarters = [row, send(row, B_ON), send(row, B_BACK), send(row, B_TWO)]

    other_later, _ = lax.optimization_barrier((other, row))
    chip = join(text_emb, other_later, weight=20.0)
    one = send(chip, Z_ONE)
    two = send(chip, Z_TWO)
    near_give = [one, two, other]
    near_keep = [send(one, CORE), send(two, CORE), text_emb]
    yh_near = normalize_all(*near_give, *near_keep)
    near = [near_part(0, weight, pos, near_ids, row, yh_near)]
    passed, near[0], *quarters[1:] = lax.optimization_barrier((two, near[0], *quarters[1:]))
    three = send(passed, Z_ONE)
    four = send(passed[:64], Z_TWO)

    near += [near_part(k, weight, pos, near_ids, quarters[k], yh_near) for k in (1, 2, 3)]
    gs, xs, parts = zip(*near)
    d_give = text_sum(0, gs, xs, near_give, "near_give")
    swapped = send(d_give, CORE)
    three, four, d_give = lax.optimization_barrier((three, four, d_give))
    far_give = [three, four]
    far_keep = [send(three, CORE), send(four, CORE)]
    yh_far = normalize_all(*far_give, *far_keep)
    near_swapped = swapped
    fs = [far_part(k, weight, pos, far_ids, xs[k], yh_far) for k in range(4)]
    d_give = text_sum(0, fs, xs, far_give, "far_give")
    swapped = send(d_give, CORE)
    d_keep = text_sum(192, fs, xs, far_keep, "far_keep")
    far_sum = add(d_keep, swapped).astype(BF16)
    far_sum, *fs = lax.optimization_barrier((far_sum, *fs))
    es = [image_sum(quarters[k], yh_far, parts[k], fs[k]) for k in range(4)]
    gs = lax.optimization_barrier((far_sum, *gs))[1:]
    d_keep = text_sum(320, gs, xs, near_keep, "near_keep")
    near_sum = add(d_keep, near_swapped)

    relay = send(far_sum, Z_TWO)
    half = add(near_sum[0:192], relay).astype(BF16)
    w1 = send(half[0:128], Z_ONE)
    w2 = send(jnp.concatenate([half[128:192], near_sum[192:256].astype(BF16)], axis=0), Z_TWO)
    to_other = add(w1[:64], w2[:64]).astype(BF16)
    last = send(to_other, CORE)
    grad_text = add(near_sum[256:320], w1[64:], w2[64:], last).astype(BF16)

    back = [send(es[1], B_BACK), send(es[2], B_ON), send(es[3], B_TWO)]
    row_sum = add(es[0], *back)
    row_half = row_sum.astype(BF16)
    home = [send(row_half[64:128], A_BACK), send(row_half[128:192], A_ON), send(row_half[192:256], A_TWO)]
    grad_image = add(row_sum[:64], *home).astype(BF16)
    return grad_image, grad_text


def solution(mesh):
    in_specs = (P(("img", "txt"), None), P(("txt", "img"), None), P("img"), P())
    out_specs = (P(("img", "txt"), None), P(("txt", "img"), None))
    return jax.shard_map(local, mesh=mesh, in_specs=in_specs, out_specs=out_specs, check_vma=False)
```

```python
import functools

import jax
import jax.numpy as jnp
import numpy as np
from jax import lax
from jax.experimental import pallas as pl
from jax.experimental.pallas import tpu as pltpu
from jax.sharding import PartitionSpec as P

temper = 32.0
offset = -2.0
epsilon = 1e-06
F32 = jnp.float32
BF16 = jnp.bfloat16
AXES = ("img", "txt")
NX, NY, NZ = 4, 4, 8
VMEM_LIMIT = 16 * 1024 * 1024


def line(z, y, x, c):
    return ((z * 2 + y // 2) * 2 + y % 2) * (NX * 2) + x * 2 + c


def make_perm(move):
    pairs = []
    for z in range(NZ):
        for y in range(NY):
            for x in range(NX):
                for c in range(2):
                    tz, ty, tx, tc = move(z, y, x, c, 1 - 2 * c)
                    pairs.append((line(z, y, x, c), line(tz % NZ, ty % NY, tx % NX, tc)))
    return pairs


CORE = make_perm(lambda z, y, x, c, s: (z, y, x, 1 - c))
Z_ONE = make_perm(lambda z, y, x, c, s: (z + s, y, x, c))
Z_TWO = make_perm(lambda z, y, x, c, s: (z + 2 * s, y, x, c))


def shift_perm(first, by):
    return make_perm(
        lambda z, y, x, c, s: (z, y, x + by, c) if (c == 0) == first else (z, y + by, x, c)
    )


A_ON, A_BACK, A_TWO = (shift_perm(True, by) for by in (1, -1, 2))
B_ON, B_BACK, B_TWO = (shift_perm(False, by) for by in (1, -1, 2))
Y_TWO = make_perm(lambda z, y, x, c, s: (z, y + 2, x, c))


def send(v, perm):
    return lax.ppermute(v, AXES, perm)


def wide_inv(raw):
    wide = raw.astype(F32)
    return wide, lax.rsqrt(jnp.sum(wide * wide, axis=1, keepdims=True) + epsilon)


def project(raw, d):
    wide, inv = wide_inv(raw)
    unit = wide * inv
    dots = jnp.sum(unit * d, axis=1, keepdims=True)
    return ((d - unit * dots) * inv).astype(BF16)


def join_kernel(*refs):
    row = 0
    for p in refs[:-1]:
        n = p.shape[0]
        refs[-1][row : row + n, :] = p[...]
        row += n


def norm_kernel(*refs):
    pieces, out = refs[:-1], refs[-1]
    row = 0
    for p in pieces:
        n = p.shape[0]
        wide, inv = wide_inv(p[...])
        out[row : row + n, :] = (wide * inv).astype(BF16)
        row += n


def setup_kernel(tab_ref, scale_ref, own_ref, across_ref, pos_ref, ids_ref, weight_ref):
    core = tab_ref[48]
    for k in range(4):
        parts = []
        for j in range(4 * k, 4 * k + 4):
            at = pl.ds(tab_ref[16 + j], 1)
            both = jnp.where(tab_ref[32 + j] == 1, own_ref[at, :], across_ref[at, :])
            parts.append(jnp.where(core == 0, both[:, :64], both[:, 64:]))
        pos_ref[k : k + 1, :] = jnp.concatenate(parts, axis=1)
    row = lax.broadcasted_iota(jnp.int32, (64, 128), 0)
    for b in range(16):
        ids_ref[b * 64 : b * 64 + 64, :] = row + tab_ref[b]
    weight_ref[...] = jnp.full(weight_ref.shape, scale_ref[0], F32)


def tile_kernel(quarter, weight_ref, pos_ref, ids_ref, xh_ref, yh_ref, g_ref):
    texts, images = g_ref.shape
    weight = weight_ref[0:1, :]
    pos = pos_ref[quarter : quarter + 1, :]
    for m in range(0, texts, 512):
        rows = slice(m, m + 512)
        logits = (
            temper
            * lax.dot_general(
                yh_ref[rows, :], xh_ref[...], (((1,), (1,)), ((), ())), preferred_element_type=F32
            )
            + offset
        )
        half = jax.nn.sigmoid(logits)
        for n in range(0, images, 128):
            cols = slice(n, n + 128)
            same = (pos[:, cols] == ids_ref[rows, :]).astype(F32)
            g_ref[rows, cols] = (weight * (half[:, cols] - same)).astype(BF16)


def image_kernel(raw_ref, yh_ref, g_ref, out_ref, d_ref):
    width = yh_ref.shape[1]
    for n in range(0, width, 384):
        d_ref[:, n : n + 384] = lax.dot_general(
            g_ref[...], yh_ref[:, n : n + 384], (((0,), (0,)), ((), ())), preferred_element_type=F32
        )
    out_ref[...] = project(raw_ref[...], d_ref[...])


def text_kernel(first, *refs):
    gs, xs, pieces = refs[:4], refs[4:8], refs[8:-2]
    out_ref, d_ref = refs[-2:]
    rows, width = out_ref.shape
    for n in range(0, width, 384):
        total = None
        for g, x in zip(gs, xs):
            part = jnp.dot(
                g[first : first + rows, :], x[:, n : n + 384], preferred_element_type=F32
            )
            total = part if total is None else total + part
        d_ref[:, n : n + 384] = total
    row = 0
    for p in pieces:
        n = p.shape[0]
        out_ref[row : row + n, :] = project(p[...], d_ref[row : row + n, :])
        row += n


VM = pl.BlockSpec(memory_space=pltpu.VMEM)
SM = pl.BlockSpec(memory_space=pltpu.SMEM)
PARAMS = pltpu.CompilerParams(vmem_limit_bytes=VMEM_LIMIT)


def sds(shape, dtype):
    return jax.ShapeDtypeStruct(shape, dtype)


WEIGHT = 0.1


def fast(*arrays):
    return [pltpu.with_memory_space_constraint(a, pltpu.VMEM) for a in arrays]


def cost(us):
    return pl.CostEstimate(flops=int(us * WEIGHT * 1.15e9), bytes_accessed=1, transcendentals=0)


def join(*pieces):
    rows = sum(p.shape[0] for p in pieces)
    width = pieces[0].shape[1]
    return pl.pallas_call(
        join_kernel,
        out_shape=sds((rows, width), BF16),
        in_specs=[VM] * len(pieces),
        out_specs=VM,
        compiler_params=PARAMS,
        cost_estimate=cost(0.3),
        name="join",
    )(*fast(*pieces))


def copy_kernel(*refs):
    half = len(refs) // 2
    for src, dst in zip(refs[:half], refs[half:]):
        dst[...] = src[...]


def fetch(*arrays, us=0.3):
    return pl.pallas_call(
        copy_kernel,
        out_shape=tuple(sds(a.shape, a.dtype) for a in arrays),
        in_specs=[VM] * len(arrays),
        out_specs=tuple([VM] * len(arrays)),
        compiler_params=PARAMS,
        cost_estimate=cost(us),
        name="fetch",
    )(*fast(*arrays))


def head_kernel(src, dst):
    dst[...] = src[: dst.shape[0], :]


def head(array, rows):
    return pl.pallas_call(
        head_kernel,
        out_shape=pltpu.VMEM((rows, array.shape[1]), array.dtype),
        in_specs=[VM],
        out_specs=VM,
        compiler_params=PARAMS,
        cost_estimate=cost(0.1),
        name="head",
    )(*fast(array))


def normalize(*pieces, us=0.8):
    rows = sum(p.shape[0] for p in pieces)
    width = pieces[0].shape[1]
    return pl.pallas_call(
        norm_kernel,
        out_shape=sds((rows, width), BF16),
        in_specs=[VM] * len(pieces),
        out_specs=VM,
        compiler_params=PARAMS,
        cost_estimate=cost(us),
        name="normalize",
    )(*fast(*pieces))


def setup(tab, scale, own, across):
    return pl.pallas_call(
        setup_kernel,
        out_shape=(sds((4, 256), jnp.int32), sds((1024, 128), jnp.int32), sds((8, 128), F32)),
        in_specs=[SM, SM, VM, VM],
        out_specs=(VM, VM, VM),
        compiler_params=PARAMS,
        cost_estimate=cost(1),
        name="setup",
    )(tab, scale, own, across)


def tile(quarter, weight, pos, ids, xh, yh):
    return pl.pallas_call(
        functools.partial(tile_kernel, quarter),
        out_shape=sds((yh.shape[0], xh.shape[0]), BF16),
        in_specs=[VM] * 5,
        out_specs=VM,
        compiler_params=PARAMS,
        cost_estimate=cost(1.3),
        name="tile",
    )(*fast(weight, pos, ids, xh, yh))


def image_sum(raw, yh, g):
    return pl.pallas_call(
        image_kernel,
        out_shape=sds(raw.shape, BF16),
        in_specs=[VM] * 3,
        out_specs=VM,
        scratch_shapes=[pltpu.VMEM(raw.shape, F32)],
        compiler_params=PARAMS,
        cost_estimate=cost(1.6),
        name="image_sum",
    )(*fast(raw, yh, g))


def text_sum(first, gs, xs, pieces, name):
    rows = sum(p.shape[0] for p in pieces)
    width = pieces[0].shape[1]
    return pl.pallas_call(
        functools.partial(text_kernel, first),
        out_shape=sds((rows, width), BF16),
        in_specs=[VM] * (8 + len(pieces)),
        out_specs=VM,
        scratch_shapes=[pltpu.VMEM((rows, width), F32)],
        compiler_params=PARAMS,
        cost_estimate=cost(rows / 230),
        name=name,
    )(*fast(*gs, *xs, *pieces))


def add(*terms):
    total = terms[0].astype(F32)
    for t in terms[1:]:
        total = total + t.astype(F32)
    return total


def local(image_emb, text_emb, positive, loss_scale):
    i, t = lax.axis_index("img"), lax.axis_index("txt")
    z, yh = i // 2, i % 2
    yl, x, c = t // 8, (t // 2) % 4, t % 2
    y = yh * 2 + yl
    s = 1 - 2 * c
    d = 1 - c

    other = send(text_emb, CORE)
    images, text_emb = fetch(image_emb, text_emb)
    chip = join(text_emb, other)
    one = send(chip, Z_ONE)
    two = send(chip, Z_TWO)
    def text_base(zz, cc):
        return ((((yl * 4 + x) * 2 + cc) * 8 + zz % 8) * 2 + yh) * 64

    at = [(z - 3 * s, c), (z - 3 * s, d), (z + 4, c)]
    at += [(z + 3 * s, d), (z + 3 * s, c), (z + 4, d)]
    at += [(z - s, c), (z - s, d), (z - 2 * s, c), (z - 2 * s, d), (z, d)]
    at += [(z + s, d), (z + s, c), (z + 2 * s, d), (z + 2 * s, c), (z, c)]
    table = [text_base(*p) for p in at]
    rows, mine = [], []
    for b in (0, -1, 1, 2):
        for a in (0, -1, 1, 2):
            yy = (y + jnp.where(c == 0, b, a)) % 4
            xx = (x + jnp.where(c == 0, a, b)) % 4
            rows.append(yy % 2 * 4 + xx)
            mine.append((yy // 2 == yh).astype(jnp.int32))
    tab = jnp.stack([v.astype(jnp.int32) for v in table + rows + mine + [c]])
    scale = (loss_scale * (temper / 16384.0)).reshape(1)
    own_pairs = positive.reshape(8, 128)
    own_pairs, two = lax.optimization_barrier((own_pairs, two))
    across_pairs = send(own_pairs, Y_TWO)
    pos, ids, weight = setup(tab, scale, own_pairs, across_pairs)

    three = send(two, Z_ONE)
    four = send(head(two, 64), Z_TWO)
    far_give = [three, four]
    far_keep = [send(three, CORE), send(four, CORE)]
    near_give = [one, two, other]
    near_keep = [send(one, CORE), send(two, CORE), text_emb]

    row = join(images, send(image_emb, A_ON), send(image_emb, A_BACK), send(image_emb, A_TWO))
    quarters = [row, send(row, B_ON), send(row, B_BACK), send(row, B_TWO)]
    xs = [normalize(quarters[0], us=0.3)] + [normalize(q, us=10) for q in quarters[1:]]

    yh_all = normalize(*far_give, *far_keep, *near_give, *near_keep)
    gs = [tile(k, weight, pos, ids, xs[k], yh_all) for k in range(4)]
    d_give = text_sum(0, gs, xs, far_give, "far_give")
    swapped = send(d_give, CORE)
    d_keep = text_sum(192, gs, xs, far_keep, "far_keep")
    far_sum = add(d_keep, swapped).astype(BF16)
    relay = send(far_sum, Z_TWO)

    far_sum, *gs = lax.optimization_barrier((far_sum, *gs))
    es = [image_sum(quarters[k], yh_all, gs[k]) for k in range(4)]
    back = [send(es[1], B_BACK), send(es[2], B_ON), send(es[3], B_TWO)]

    _, *gs = lax.optimization_barrier((es[3], *gs))
    d_give = text_sum(384, gs, xs, near_give, "near_give")
    swapped = send(d_give, CORE)
    d_keep = text_sum(704, gs, xs, near_keep, "near_keep")
    near_sum = add(d_keep, swapped)
    (relay,) = fetch(relay, us=40)
    half = add(near_sum[0:192], relay).astype(BF16)
    own_sum, half = lax.optimization_barrier((es[0], half))
    row_sum = add(own_sum, *back)
    row_half = row_sum.astype(BF16)
    home = [send(row_half[64:128], A_BACK), send(row_half[128:192], A_ON), send(row_half[192:256], A_TWO)]
    grad_image = add(row_sum[:64], *home).astype(BF16)

    w1 = send(half[0:128], Z_ONE)
    w2 = send(jnp.concatenate([half[128:192], near_sum[192:256].astype(BF16)], axis=0), Z_TWO)
    w1, w2 = fetch(w1, w2, us=40)
    to_other = add(w1[:64], w2[:64]).astype(BF16)
    last = send(to_other, CORE)
    grad_text = add(near_sum[256:320], w1[64:], w2[64:], last).astype(BF16)
    return grad_image, grad_text


def solution(mesh):
    in_specs = (P(("img", "txt"), None), P(("txt", "img"), None), P("img"), P())
    out_specs = (P(("img", "txt"), None), P(("txt", "img"), None))
    return jax.shard_map(local, mesh=mesh, in_specs=in_specs, out_specs=out_specs, check_vma=False)
```

```python
import functools

import jax
import jax.numpy as jnp
import numpy as np
from jax import lax
from jax.experimental import pallas as pl
from jax.experimental.pallas import tpu as pltpu
from jax.sharding import PartitionSpec as P

temper = 32.0
offset = -2.0
epsilon = 1e-06
F32 = jnp.float32
BF16 = jnp.bfloat16
AXES = ("img", "txt")
NX, NY, NZ = 4, 4, 8
VMEM_LIMIT = 16 * 1024 * 1024


def line(z, y, x, c):
    return ((z * 2 + y // 2) * 2 + y % 2) * (NX * 2) + x * 2 + c


def make_perm(move):
    pairs = []
    for z in range(NZ):
        for y in range(NY):
            for x in range(NX):
                for c in range(2):
                    tz, ty, tx, tc = move(z, y, x, c, 1 - 2 * c)
                    pairs.append((line(z, y, x, c), line(tz % NZ, ty % NY, tx % NX, tc)))
    return pairs


CORE = make_perm(lambda z, y, x, c, s: (z, y, x, 1 - c))
Z_ONE = make_perm(lambda z, y, x, c, s: (z + s, y, x, c))
Z_TWO = make_perm(lambda z, y, x, c, s: (z + 2 * s, y, x, c))


def shift_perm(first, by):
    return make_perm(
        lambda z, y, x, c, s: (z, y, x + by, c) if (c == 0) == first else (z, y + by, x, c)
    )


A_ON, A_BACK, A_TWO = (shift_perm(True, by) for by in (1, -1, 2))
B_ON, B_BACK, B_TWO = (shift_perm(False, by) for by in (1, -1, 2))
Y_TWO = make_perm(lambda z, y, x, c, s: (z, y + 2, x, c))


def send(v, perm):
    return lax.ppermute(v, AXES, perm)


def wide_inv(raw):
    wide = raw.astype(F32)
    return wide, lax.rsqrt(jnp.sum(wide * wide, axis=1, keepdims=True) + epsilon)


def project(raw, d):
    wide, inv = wide_inv(raw)
    unit = wide * inv
    dots = jnp.sum(unit * d, axis=1, keepdims=True)
    return ((d - unit * dots) * inv).astype(BF16)


def join_kernel(*refs):
    row = 0
    for p in refs[:-1]:
        n = p.shape[0]
        refs[-1][row : row + n, :] = p[...]
        row += n


def norm_kernel(*refs):
    pieces, out = refs[:-1], refs[-1]
    row = 0
    for p in pieces:
        n = p.shape[0]
        wide, inv = wide_inv(p[...])
        out[row : row + n, :] = (wide * inv).astype(BF16)
        row += n


def setup_kernel(tab_ref, scale_ref, own_ref, across_ref, pos_ref, ids_ref, weight_ref):
    core = tab_ref[48]
    for k in range(4):
        parts = []
        for j in range(4 * k, 4 * k + 4):
            at = pl.ds(tab_ref[16 + j], 1)
            both = jnp.where(tab_ref[32 + j] == 1, own_ref[at, :], across_ref[at, :])
            parts.append(jnp.where(core == 0, both[:, :64], both[:, 64:]))
        pos_ref[k : k + 1, :] = jnp.concatenate(parts, axis=1)
    row = lax.broadcasted_iota(jnp.int32, (64, 128), 0)
    for b in range(16):
        ids_ref[b * 64 : b * 64 + 64, :] = row + tab_ref[b]
    weight_ref[...] = jnp.full(weight_ref.shape, scale_ref[0], F32)


def tile_kernel(quarter, weight_ref, pos_ref, ids_ref, xh_ref, yh_ref, g_ref):
    texts, images = g_ref.shape
    weight = weight_ref[0:1, :]
    pos = pos_ref[quarter : quarter + 1, :]
    for m in range(0, texts, 512):
        rows = slice(m, m + 512)
        logits = (
            temper
            * lax.dot_general(
                yh_ref[rows, :], xh_ref[...], (((1,), (1,)), ((), ())), preferred_element_type=F32
            )
            + offset
        )
        half = jax.nn.sigmoid(logits)
        for n in range(0, images, 128):
            cols = slice(n, n + 128)
            same = (pos[:, cols] == ids_ref[rows, :]).astype(F32)
            g_ref[rows, cols] = (weight * (half[:, cols] - same)).astype(BF16)


def image_kernel(raw_ref, yh_ref, g_ref, out_ref, d_ref):
    width = yh_ref.shape[1]
    for n in range(0, width, 384):
        d_ref[:, n : n + 384] = lax.dot_general(
            g_ref[...], yh_ref[:, n : n + 384], (((0,), (0,)), ((), ())), preferred_element_type=F32
        )
    out_ref[...] = project(raw_ref[...], d_ref[...])


def text_kernel(first, spans, *refs):
    gs, xs, pieces = refs[:4], refs[4:8], refs[8:-2]
    out_ref, d_ref = refs[-2:]
    rows, width = out_ref.shape
    for n in range(0, width, 384):
        total = None
        for g, x in zip(gs, xs):
            part = jnp.dot(
                g[first : first + rows, :], x[:, n : n + 384], preferred_element_type=F32
            )
            total = part if total is None else total + part
        d_ref[:, n : n + 384] = total
    row = 0
    for p, (low, high) in zip(pieces, spans):
        n = high - low
        out_ref[row : row + n, :] = project(p[low:high, :], d_ref[row : row + n, :])
        row += n


VM = pl.BlockSpec(memory_space=pltpu.VMEM)
SM = pl.BlockSpec(memory_space=pltpu.SMEM)
PARAMS = pltpu.CompilerParams(vmem_limit_bytes=VMEM_LIMIT)


def sds(shape, dtype):
    return jax.ShapeDtypeStruct(shape, dtype)


WEIGHT = 0.1


def fast(*arrays):
    return [pltpu.with_memory_space_constraint(a, pltpu.VMEM) for a in arrays]


def cost(us):
    return pl.CostEstimate(flops=int(us * WEIGHT * 1.15e9), bytes_accessed=1, transcendentals=0)


def join(*pieces):
    rows = sum(p.shape[0] for p in pieces)
    width = pieces[0].shape[1]
    return pl.pallas_call(
        join_kernel,
        out_shape=sds((rows, width), BF16),
        in_specs=[VM] * len(pieces),
        out_specs=VM,
        compiler_params=PARAMS,
        cost_estimate=cost(0.3),
        name="join",
    )(*fast(*pieces))


def copy_kernel(*refs):
    half = len(refs) // 2
    for src, dst in zip(refs[:half], refs[half:]):
        dst[...] = src[...]


def fetch(*arrays, us=0.3):
    return pl.pallas_call(
        copy_kernel,
        out_shape=tuple(sds(a.shape, a.dtype) for a in arrays),
        in_specs=[VM] * len(arrays),
        out_specs=tuple([VM] * len(arrays)),
        compiler_params=PARAMS,
        cost_estimate=cost(us),
        name="fetch",
    )(*fast(*arrays))


def head_kernel(src, dst):
    dst[...] = src[: dst.shape[0], :]


def head(array, rows):
    return pl.pallas_call(
        head_kernel,
        out_shape=pltpu.VMEM((rows, array.shape[1]), array.dtype),
        in_specs=[VM],
        out_specs=VM,
        compiler_params=PARAMS,
        cost_estimate=cost(0.1),
        name="head",
    )(*fast(array))


def normalize(*pieces, us=0.8):
    rows = sum(p.shape[0] for p in pieces)
    width = pieces[0].shape[1]
    return pl.pallas_call(
        norm_kernel,
        out_shape=sds((rows, width), BF16),
        in_specs=[VM] * len(pieces),
        out_specs=VM,
        compiler_params=PARAMS,
        cost_estimate=cost(us),
        name="normalize",
    )(*fast(*pieces))


def setup(tab, scale, own, across):
    return pl.pallas_call(
        setup_kernel,
        out_shape=(sds((4, 256), jnp.int32), sds((1024, 128), jnp.int32), sds((8, 128), F32)),
        in_specs=[SM, SM, VM, VM],
        out_specs=(VM, VM, VM),
        compiler_params=PARAMS,
        cost_estimate=cost(1),
        name="setup",
    )(tab, scale, own, across)


def tile(quarter, weight, pos, ids, xh, yh):
    return pl.pallas_call(
        functools.partial(tile_kernel, quarter),
        out_shape=sds((yh.shape[0], xh.shape[0]), BF16),
        in_specs=[VM] * 5,
        out_specs=VM,
        compiler_params=PARAMS,
        cost_estimate=cost(1.3),
        name="tile",
    )(*fast(weight, pos, ids, xh, yh))


def image_sum(raw, yh, g):
    return pl.pallas_call(
        image_kernel,
        out_shape=sds(raw.shape, BF16),
        in_specs=[VM] * 3,
        out_specs=VM,
        scratch_shapes=[pltpu.VMEM(raw.shape, F32)],
        compiler_params=PARAMS,
        cost_estimate=cost(1.6),
        name="image_sum",
    )(*fast(raw, yh, g))


def text_sum(first, gs, xs, pieces, name):
    arrays = [p[0] for p in pieces]
    spans = tuple((low, high) for _, low, high in pieces)
    rows = sum(high - low for low, high in spans)
    width = arrays[0].shape[1]
    return pl.pallas_call(
        functools.partial(text_kernel, first, spans),
        out_shape=sds((rows, width), BF16),
        in_specs=[VM] * (8 + len(arrays)),
        out_specs=VM,
        scratch_shapes=[pltpu.VMEM((rows, width), F32)],
        compiler_params=PARAMS,
        cost_estimate=cost(rows / 230),
        name=name,
    )(*fast(*gs, *xs, *arrays))


def add(*terms):
    total = terms[0].astype(F32)
    for t in terms[1:]:
        total = total + t.astype(F32)
    return total


def local(image_emb, text_emb, positive, loss_scale):
    i, t = lax.axis_index("img"), lax.axis_index("txt")
    z, yh = i // 2, i % 2
    yl, x, c = t // 8, (t // 2) % 4, t % 2
    y = yh * 2 + yl
    s = 1 - 2 * c
    d = 1 - c

    other = send(text_emb, CORE)
    images, text_emb = fetch(image_emb, text_emb)
    chip = join(text_emb, other)
    one = send(chip, Z_ONE)
    two = send(chip, Z_TWO)
    three = send(two, Z_ONE)
    four = send(head(two, 64), Z_TWO)

    def text_base(zz, cc):
        return ((((yl * 4 + x) * 2 + cc) * 8 + zz % 8) * 2 + yh) * 64

    at = [(z - 3 * s, c), (z - 3 * s, d), (z + 4, c)]
    at += [(z - s, c), (z - s, d), (z - 2 * s, c), (z - 2 * s, d), (z, d)]
    at += [(z + 3 * s, d), (z + 3 * s, c), (z + 4, d)]
    at += [(z + s, d), (z + s, c), (z + 2 * s, d), (z + 2 * s, c), (z, c)]
    table = [text_base(*p) for p in at]
    rows, mine = [], []
    for b in (0, -1, 1, 2):
        for a in (0, -1, 1, 2):
            yy = (y + jnp.where(c == 0, b, a)) % 4
            xx = (x + jnp.where(c == 0, a, b)) % 4
            rows.append(yy % 2 * 4 + xx)
            mine.append((yy // 2 == yh).astype(jnp.int32))
    tab = jnp.stack([v.astype(jnp.int32) for v in table + rows + mine + [c]])
    scale = (loss_scale * (temper / 16384.0)).reshape(1)
    own_pairs = positive.reshape(8, 128)
    own_pairs, three = lax.optimization_barrier((own_pairs, three))
    across_pairs = send(own_pairs, Y_TWO)
    pos, ids, weight = setup(tab, scale, own_pairs, across_pairs)

    give = join(three, four, one, two)
    keep = send(give, CORE)
    far_give, near_give = [(give, 0, 192)], [(give, 192, 448), (other, 0, 64)]
    far_keep, near_keep = [(keep, 0, 192)], [(keep, 192, 448), (text_emb, 0, 64)]

    row = join(images, send(image_emb, A_ON), send(image_emb, A_BACK), send(image_emb, A_TWO))
    quarters = [row, send(row, B_ON), send(row, B_BACK), send(row, B_TWO)]
    xs = [normalize(quarters[0], us=0.3)] + [normalize(q, us=40) for q in quarters[1:]]

    yh_all = normalize(give, other, keep, text_emb)
    gs = [tile(k, weight, pos, ids, xs[k], yh_all) for k in range(4)]
    d_give = text_sum(0, gs, xs, far_give, "far_give")
    swapped = send(d_give, CORE)
    d_keep = text_sum(512, gs, xs, far_keep, "far_keep")
    far_sum = add(d_keep, swapped).astype(BF16)
    relay = send(far_sum, Z_TWO)

    far_sum, *gs = lax.optimization_barrier((far_sum, *gs))
    es = [image_sum(quarters[k], yh_all, gs[k]) for k in range(4)]
    back = [send(es[1], B_BACK), send(es[2], B_ON), send(es[3], B_TWO)]

    _, *gs = lax.optimization_barrier((es[3], *gs))
    d_give = text_sum(192, gs, xs, near_give, "near_give")
    swapped = send(d_give, CORE)
    d_keep = text_sum(704, gs, xs, near_keep, "near_keep")
    near_sum = add(d_keep, swapped)
    (relay,) = fetch(relay, us=40)
    half = add(near_sum[0:192], relay).astype(BF16)
    own_sum, half = lax.optimization_barrier((es[0], half))
    row_sum = add(own_sum, *back)
    row_half = row_sum.astype(BF16)
    home = [send(row_half[64:128], A_BACK), send(row_half[128:192], A_ON), send(row_half[192:256], A_TWO)]
    grad_image = add(row_sum[:64], *home).astype(BF16)

    w1 = send(half[0:128], Z_ONE)
    w2 = send(jnp.concatenate([half[128:192], near_sum[192:256].astype(BF16)], axis=0), Z_TWO)
    w1, w2 = fetch(w1, w2, us=40)
    to_other = add(w1[:64], w2[:64]).astype(BF16)
    last = send(to_other, CORE)
    grad_text = add(near_sum[256:320], w1[64:], w2[64:], last).astype(BF16)
    return grad_image, grad_text


def solution(mesh):
    in_specs = (P(("img", "txt"), None), P(("txt", "img"), None), P("img"), P())
    out_specs = (P(("img", "txt"), None), P(("txt", "img"), None))
    return jax.shard_map(local, mesh=mesh, in_specs=in_specs, out_specs=out_specs, check_vma=False)
```

```python
import functools

import jax
import jax.numpy as jnp
import numpy as np
from jax import lax
from jax.experimental import pallas as pl
from jax.experimental.pallas import tpu as pltpu
from jax.sharding import PartitionSpec as P

temper = 32.0
offset = -2.0
epsilon = 1e-06
F32 = jnp.float32
BF16 = jnp.bfloat16
AXES = ("img", "txt")
NX, NY, NZ = 4, 4, 8
VMEM_LIMIT = 16 * 1024 * 1024


def line(z, y, x, c):
    return ((z * 2 + y // 2) * 2 + y % 2) * (NX * 2) + x * 2 + c


def make_perm(move):
    pairs = []
    for z in range(NZ):
        for y in range(NY):
            for x in range(NX):
                for c in range(2):
                    tz, ty, tx, tc = move(z, y, x, c, 1 - 2 * c)
                    pairs.append((line(z, y, x, c), line(tz % NZ, ty % NY, tx % NX, tc)))
    return pairs


CORE = make_perm(lambda z, y, x, c, s: (z, y, x, 1 - c))
Z_ONE = make_perm(lambda z, y, x, c, s: (z + s, y, x, c))
Z_TWO = make_perm(lambda z, y, x, c, s: (z + 2 * s, y, x, c))


def shift_perm(first, by):
    return make_perm(
        lambda z, y, x, c, s: (z, y, x + by, c) if (c == 0) == first else (z, y + by, x, c)
    )


A_ON, A_BACK, A_TWO = (shift_perm(True, by) for by in (1, -1, 2))
B_ON, B_BACK, B_TWO = (shift_perm(False, by) for by in (1, -1, 2))
Y_TWO = make_perm(lambda z, y, x, c, s: (z, y + 2, x, c))


def send(v, perm):
    return lax.ppermute(v, AXES, perm)


def wide_inv(raw):
    wide = raw.astype(F32)
    return wide, lax.rsqrt(jnp.sum(wide * wide, axis=1, keepdims=True) + epsilon)


def project(raw, d):
    wide, inv = wide_inv(raw)
    unit = wide * inv
    dots = jnp.sum(unit * d, axis=1, keepdims=True)
    return ((d - unit * dots) * inv).astype(BF16)


def join_kernel(*refs):
    row = 0
    for p in refs[:-1]:
        n = p.shape[0]
        refs[-1][row : row + n, :] = p[...]
        row += n


def norm_kernel(*refs):
    pieces, out = refs[:-1], refs[-1]
    row = 0
    for p in pieces:
        n = p.shape[0]
        wide, inv = wide_inv(p[...])
        out[row : row + n, :] = (wide * inv).astype(BF16)
        row += n


def setup_kernel(tab_ref, scale_ref, own_ref, across_ref, pos_ref, ids_ref, weight_ref):
    core = tab_ref[48]
    for k in range(4):
        parts = []
        for j in range(4 * k, 4 * k + 4):
            at = pl.ds(tab_ref[16 + j], 1)
            both = jnp.where(tab_ref[32 + j] == 1, own_ref[at, :], across_ref[at, :])
            parts.append(jnp.where(core == 0, both[:, :64], both[:, 64:]))
        pos_ref[k : k + 1, :] = jnp.concatenate(parts, axis=1)
    row = lax.broadcasted_iota(jnp.int32, (64, 128), 0)
    for b in range(16):
        ids_ref[b * 64 : b * 64 + 64, :] = row + tab_ref[b]
    weight_ref[...] = jnp.full(weight_ref.shape, scale_ref[0], F32)


def tile_kernel(quarter, weight_ref, pos_ref, ids_ref, xh_ref, yh_ref, g_ref):
    texts, images = g_ref.shape
    weight = weight_ref[0:1, :]
    pos = pos_ref[quarter : quarter + 1, :]
    for m in range(0, texts, 512):
        rows = slice(m, m + 512)
        logits = (
            temper
            * lax.dot_general(
                yh_ref[rows, :], xh_ref[...], (((1,), (1,)), ((), ())), preferred_element_type=F32
            )
            + offset
        )
        half = jax.nn.sigmoid(logits)
        for n in range(0, images, 128):
            cols = slice(n, n + 128)
            same = (pos[:, cols] == ids_ref[rows, :]).astype(F32)
            g_ref[rows, cols] = (weight * (half[:, cols] - same)).astype(BF16)


def image_kernel(raw_ref, yh_ref, g_ref, out_ref, d_ref):
    width = yh_ref.shape[1]
    for n in range(0, width, 384):
        d_ref[:, n : n + 384] = lax.dot_general(
            g_ref[...], yh_ref[:, n : n + 384], (((0,), (0,)), ((), ())), preferred_element_type=F32
        )
    out_ref[...] = project(raw_ref[...], d_ref[...])


def text_kernel(first, spans, *refs):
    gs, xs, pieces = refs[:4], refs[4:8], refs[8:-2]
    out_ref, d_ref = refs[-2:]
    rows, width = out_ref.shape
    for n in range(0, width, 384):
        total = None
        for g, x in zip(gs, xs):
            part = jnp.dot(
                g[first : first + rows, :], x[:, n : n + 384], preferred_element_type=F32
            )
            total = part if total is None else total + part
        d_ref[:, n : n + 384] = total
    row = 0
    for p, (low, high) in zip(pieces, spans):
        n = high - low
        out_ref[row : row + n, :] = project(p[low:high, :], d_ref[row : row + n, :])
        row += n


VM = pl.BlockSpec(memory_space=pltpu.VMEM)
SM = pl.BlockSpec(memory_space=pltpu.SMEM)
PARAMS = pltpu.CompilerParams(vmem_limit_bytes=VMEM_LIMIT)


def sds(shape, dtype):
    return jax.ShapeDtypeStruct(shape, dtype)


WEIGHT = 0.15


def fast(*arrays):
    return [pltpu.with_memory_space_constraint(a, pltpu.VMEM) for a in arrays]


def cost(us):
    return pl.CostEstimate(flops=int(us * WEIGHT * 1.15e9), bytes_accessed=1, transcendentals=0)


def join(*pieces):
    rows = sum(p.shape[0] for p in pieces)
    width = pieces[0].shape[1]
    return pl.pallas_call(
        join_kernel,
        out_shape=sds((rows, width), BF16),
        in_specs=[VM] * len(pieces),
        out_specs=VM,
        compiler_params=PARAMS,
        cost_estimate=cost(0.3),
        name="join",
    )(*fast(*pieces))


def copy_kernel(*refs):
    half = len(refs) // 2
    for src, dst in zip(refs[:half], refs[half:]):
        dst[...] = src[...]


def fetch(*arrays, us=0.3):
    return pl.pallas_call(
        copy_kernel,
        out_shape=tuple(sds(a.shape, a.dtype) for a in arrays),
        in_specs=[VM] * len(arrays),
        out_specs=tuple([VM] * len(arrays)),
        compiler_params=PARAMS,
        cost_estimate=cost(us),
        name="fetch",
    )(*fast(*arrays))


def head_kernel(src, dst):
    dst[...] = src[: dst.shape[0], :]


def head(array, rows):
    return pl.pallas_call(
        head_kernel,
        out_shape=pltpu.VMEM((rows, array.shape[1]), array.dtype),
        in_specs=[VM],
        out_specs=VM,
        compiler_params=PARAMS,
        cost_estimate=cost(0.1),
        name="head",
    )(*fast(array))


def normalize(*pieces, us=0.8):
    rows = sum(p.shape[0] for p in pieces)
    width = pieces[0].shape[1]
    return pl.pallas_call(
        norm_kernel,
        out_shape=sds((rows, width), BF16),
        in_specs=[VM] * len(pieces),
        out_specs=VM,
        compiler_params=PARAMS,
        cost_estimate=cost(us),
        name="normalize",
    )(*fast(*pieces))


def setup(tab, scale, own, across):
    return pl.pallas_call(
        setup_kernel,
        out_shape=(sds((4, 256), jnp.int32), sds((1024, 128), jnp.int32), sds((8, 128), F32)),
        in_specs=[SM, SM, VM, VM],
        out_specs=(VM, VM, VM),
        compiler_params=PARAMS,
        cost_estimate=cost(1),
        name="setup",
    )(tab, scale, own, across)


def tile(quarter, weight, pos, ids, xh, yh):
    return pl.pallas_call(
        functools.partial(tile_kernel, quarter),
        out_shape=sds((yh.shape[0], xh.shape[0]), BF16),
        in_specs=[VM] * 5,
        out_specs=VM,
        compiler_params=PARAMS,
        cost_estimate=cost(1.3),
        name="tile",
    )(*fast(weight, pos, ids, xh, yh))


def image_sum(raw, yh, g):
    return pl.pallas_call(
        image_kernel,
        out_shape=sds(raw.shape, BF16),
        in_specs=[VM] * 3,
        out_specs=VM,
        scratch_shapes=[pltpu.VMEM(raw.shape, F32)],
        compiler_params=PARAMS,
        cost_estimate=cost(1.6),
        name="image_sum",
    )(*fast(raw, yh, g))


def text_sum(first, gs, xs, pieces, name):
    arrays = [p[0] for p in pieces]
    spans = tuple((low, high) for _, low, high in pieces)
    rows = sum(high - low for low, high in spans)
    width = arrays[0].shape[1]
    return pl.pallas_call(
        functools.partial(text_kernel, first, spans),
        out_shape=sds((rows, width), BF16),
        in_specs=[VM] * (8 + len(arrays)),
        out_specs=VM,
        scratch_shapes=[pltpu.VMEM((rows, width), F32)],
        compiler_params=PARAMS,
        cost_estimate=cost(rows / 230),
        name=name,
    )(*fast(*gs, *xs, *arrays))


def add(*terms):
    total = terms[0].astype(F32)
    for t in terms[1:]:
        total = total + t.astype(F32)
    return total


def local(image_emb, text_emb, positive, loss_scale):
    i, t = lax.axis_index("img"), lax.axis_index("txt")
    z, yh = i // 2, i % 2
    yl, x, c = t // 8, (t // 2) % 4, t % 2
    y = yh * 2 + yl
    s = 1 - 2 * c
    d = 1 - c

    other = send(text_emb, CORE)
    images, text_emb = fetch(image_emb, text_emb)
    chip = join(text_emb, other)
    one = send(chip, Z_ONE)
    two = send(chip, Z_TWO)
    three = send(two, Z_ONE)
    four = send(head(two, 64), Z_TWO)

    def text_base(zz, cc):
        return ((((yl * 4 + x) * 2 + cc) * 8 + zz % 8) * 2 + yh) * 64

    at = [(z - 3 * s, c), (z - 3 * s, d), (z + 4, c)]
    at += [(z - s, c), (z - s, d), (z - 2 * s, c), (z - 2 * s, d), (z, d)]
    at += [(z + 3 * s, d), (z + 3 * s, c), (z + 4, d)]
    at += [(z + s, d), (z + s, c), (z + 2 * s, d), (z + 2 * s, c), (z, c)]
    table = [text_base(*p) for p in at]
    rows, mine = [], []
    for b in (0, -1, 1, 2):
        for a in (0, -1, 1, 2):
            yy = (y + jnp.where(c == 0, b, a)) % 4
            xx = (x + jnp.where(c == 0, a, b)) % 4
            rows.append(yy % 2 * 4 + xx)
            mine.append((yy // 2 == yh).astype(jnp.int32))
    tab = jnp.stack([v.astype(jnp.int32) for v in table + rows + mine + [c]])
    scale = (loss_scale * (temper / 16384.0)).reshape(1)
    own_pairs = positive.reshape(8, 128)
    own_pairs, three = lax.optimization_barrier((own_pairs, three))
    across_pairs = send(own_pairs, Y_TWO)
    pos, ids, weight = setup(tab, scale, own_pairs, across_pairs)

    give = join(three, four, one, two)
    keep = send(give, CORE)
    far_give, near_give = [(give, 0, 192)], [(give, 192, 448), (other, 0, 64)]
    far_keep, near_keep = [(keep, 0, 192)], [(keep, 192, 448), (text_emb, 0, 64)]

    row = join(images, send(image_emb, A_ON), send(image_emb, A_BACK), send(image_emb, A_TWO))
    quarters = [row, send(row, B_ON), send(row, B_BACK), send(row, B_TWO)]
    xs = [normalize(quarters[0], us=0.3)] + [normalize(q, us=40) for q in quarters[1:]]

    yh_all = normalize(give, other, keep, text_emb)
    gs = [tile(k, weight, pos, ids, xs[k], yh_all) for k in range(4)]
    d_give = text_sum(0, gs, xs, far_give, "far_give")
    swapped = send(d_give, CORE)
    d_keep = text_sum(512, gs, xs, far_keep, "far_keep")
    far_sum = add(d_keep, swapped).astype(BF16)
    relay = send(far_sum, Z_TWO)

    far_sum, *gs = lax.optimization_barrier((far_sum, *gs))
    es = [image_sum(quarters[k], yh_all, gs[k]) for k in range(4)]
    back = [send(es[1], B_BACK), send(es[2], B_ON), send(es[3], B_TWO)]

    _, *gs = lax.optimization_barrier((es[3], *gs))
    d_give = text_sum(192, gs, xs, near_give, "near_give")
    swapped = send(d_give, CORE)
    d_keep = text_sum(704, gs, xs, near_keep, "near_keep")
    near_sum = add(d_keep, swapped)
    (relay,) = fetch(relay, us=40)
    half = add(near_sum[0:192], relay).astype(BF16)
    own_sum, half = lax.optimization_barrier((es[0], half))
    row_sum = add(own_sum, *back)
    row_half = row_sum.astype(BF16)
    home = [send(row_half[64:128], A_BACK), send(row_half[128:192], A_ON), send(row_half[192:256], A_TWO)]
    grad_image = add(row_sum[:64], *home).astype(BF16)

    w1 = send(half[0:128], Z_ONE)
    w2 = send(jnp.concatenate([half[128:192], near_sum[192:256].astype(BF16)], axis=0), Z_TWO)
    w1, w2 = fetch(w1, w2, us=40)
    to_other = add(w1[:64], w2[:64]).astype(BF16)
    last = send(to_other, CORE)
    grad_text = add(near_sum[256:320], w1[64:], w2[64:], last).astype(BF16)
    return grad_image, grad_text


def solution(mesh):
    in_specs = (P(("img", "txt"), None), P(("txt", "img"), None), P("img"), P())
    out_specs = (P(("img", "txt"), None), P(("txt", "img"), None))
    return jax.shard_map(local, mesh=mesh, in_specs=in_specs, out_specs=out_specs, check_vma=False)
```

```python
import functools

import jax
import jax.numpy as jnp
import numpy as np
from jax import lax
from jax.experimental import pallas as pl
from jax.experimental.pallas import tpu as pltpu
from jax.sharding import PartitionSpec as P

temper = 32.0
offset = -2.0
epsilon = 1e-06
F32 = jnp.float32
BF16 = jnp.bfloat16
AXES = ("img", "txt")
NX, NY, NZ = 4, 4, 8
VMEM_LIMIT = 16 * 1024 * 1024


def line(z, y, x, c):
    return ((z * 2 + y // 2) * 2 + y % 2) * (NX * 2) + x * 2 + c


def make_perm(move):
    pairs = []
    for z in range(NZ):
        for y in range(NY):
            for x in range(NX):
                for c in range(2):
                    tz, ty, tx, tc = move(z, y, x, c, 1 - 2 * c)
                    pairs.append((line(z, y, x, c), line(tz % NZ, ty % NY, tx % NX, tc)))
    return pairs


CORE = make_perm(lambda z, y, x, c, s: (z, y, x, 1 - c))
Z_ONE = make_perm(lambda z, y, x, c, s: (z + s, y, x, c))
Z_TWO = make_perm(lambda z, y, x, c, s: (z + 2 * s, y, x, c))


def shift_perm(first, by):
    return make_perm(
        lambda z, y, x, c, s: (z, y, x + by, c) if (c == 0) == first else (z, y + by, x, c)
    )


A_ON, A_BACK, A_TWO = (shift_perm(True, by) for by in (1, -1, 2))
B_ON, B_BACK, B_TWO = (shift_perm(False, by) for by in (1, -1, 2))
Y_TWO = make_perm(lambda z, y, x, c, s: (z, y + 2, x, c))


def send(v, perm):
    return lax.ppermute(v, AXES, perm)


def wide_inv(raw):
    wide = raw.astype(F32)
    return wide, lax.rsqrt(jnp.sum(wide * wide, axis=1, keepdims=True) + epsilon)


def project(raw, d):
    wide, inv = wide_inv(raw)
    unit = wide * inv
    dots = jnp.sum(unit * d, axis=1, keepdims=True)
    return ((d - unit * dots) * inv).astype(BF16)


def join_kernel(*refs):
    row = 0
    for p in refs[:-1]:
        n = p.shape[0]
        refs[-1][row : row + n, :] = p[...]
        row += n


def norm_kernel(*refs):
    pieces, out = refs[:-1], refs[-1]
    row = 0
    for p in pieces:
        n = p.shape[0]
        wide, inv = wide_inv(p[...])
        out[row : row + n, :] = (wide * inv).astype(BF16)
        row += n


def setup_kernel(tab_ref, scale_ref, own_ref, across_ref, pos_ref, ids_ref, weight_ref):
    core = tab_ref[48]
    for k in range(4):
        parts = []
        for j in range(4 * k, 4 * k + 4):
            at = pl.ds(tab_ref[16 + j], 1)
            both = jnp.where(tab_ref[32 + j] == 1, own_ref[at, :], across_ref[at, :])
            parts.append(jnp.where(core == 0, both[:, :64], both[:, 64:]))
        pos_ref[k : k + 1, :] = jnp.concatenate(parts, axis=1)
    row = lax.broadcasted_iota(jnp.int32, (64, 128), 0)
    for b in range(16):
        ids_ref[b * 64 : b * 64 + 64, :] = row + tab_ref[b]
    weight_ref[...] = jnp.full(weight_ref.shape, scale_ref[0], F32)


def tile_kernel(quarter, weight_ref, pos_ref, ids_ref, xh_ref, yh_ref, g_ref):
    texts, images = g_ref.shape
    weight = weight_ref[0:1, :]
    pos = pos_ref[quarter : quarter + 1, :]
    for m in range(0, texts, 512):
        rows = slice(m, m + 512)
        logits = (
            temper
            * lax.dot_general(
                yh_ref[rows, :], xh_ref[...], (((1,), (1,)), ((), ())), preferred_element_type=F32
            )
            + offset
        )
        half = jax.nn.sigmoid(logits)
        for n in range(0, images, 128):
            cols = slice(n, n + 128)
            same = (pos[:, cols] == ids_ref[rows, :]).astype(F32)
            g_ref[rows, cols] = (weight * (half[:, cols] - same)).astype(BF16)


def image_kernel(raw_ref, yh_ref, g_ref, out_ref, d_ref):
    width = yh_ref.shape[1]
    for n in range(0, width, 384):
        d_ref[:, n : n + 384] = lax.dot_general(
            g_ref[...], yh_ref[:, n : n + 384], (((0,), (0,)), ((), ())), preferred_element_type=F32
        )
    out_ref[...] = project(raw_ref[...], d_ref[...])


def text_kernel(first, spans, *refs):
    gs, xs, pieces = refs[:4], refs[4:8], refs[8:-2]
    out_ref, d_ref = refs[-2:]
    rows, width = out_ref.shape
    for n in range(0, width, 384):
        total = None
        for g, x in zip(gs, xs):
            part = jnp.dot(
                g[first : first + rows, :], x[:, n : n + 384], preferred_element_type=F32
            )
            total = part if total is None else total + part
        d_ref[:, n : n + 384] = total
    row = 0
    for p, (low, high) in zip(pieces, spans):
        n = high - low
        out_ref[row : row + n, :] = project(p[low:high, :], d_ref[row : row + n, :])
        row += n


VM = pl.BlockSpec(memory_space=pltpu.VMEM)
SM = pl.BlockSpec(memory_space=pltpu.SMEM)
PARAMS = pltpu.CompilerParams(vmem_limit_bytes=VMEM_LIMIT)


def sds(shape, dtype):
    return jax.ShapeDtypeStruct(shape, dtype)


WEIGHT = 0.15


def fast(*arrays):
    return [pltpu.with_memory_space_constraint(a, pltpu.VMEM) for a in arrays]


def cost(us):
    return pl.CostEstimate(flops=int(us * WEIGHT * 1.15e9), bytes_accessed=1, transcendentals=0)


def join(*pieces):
    rows = sum(p.shape[0] for p in pieces)
    width = pieces[0].shape[1]
    return pl.pallas_call(
        join_kernel,
        out_shape=sds((rows, width), BF16),
        in_specs=[VM] * len(pieces),
        out_specs=VM,
        compiler_params=PARAMS,
        cost_estimate=cost(0.3),
        name="join",
    )(*fast(*pieces))


def copy_kernel(*refs):
    half = len(refs) // 2
    for src, dst in zip(refs[:half], refs[half:]):
        dst[...] = src[...]


def fetch(*arrays, us=0.3):
    return pl.pallas_call(
        copy_kernel,
        out_shape=tuple(sds(a.shape, a.dtype) for a in arrays),
        in_specs=[VM] * len(arrays),
        out_specs=tuple([VM] * len(arrays)),
        compiler_params=PARAMS,
        cost_estimate=cost(us),
        name="fetch",
    )(*fast(*arrays))


def head_kernel(src, dst):
    dst[...] = src[: dst.shape[0], :]


def head(array, rows):
    return pl.pallas_call(
        head_kernel,
        out_shape=pltpu.VMEM((rows, array.shape[1]), array.dtype),
        in_specs=[VM],
        out_specs=VM,
        compiler_params=PARAMS,
        cost_estimate=cost(0.1),
        name="head",
    )(*fast(array))


def norm_each_kernel(*refs):
    half = len(refs) // 2
    for src, dst in zip(refs[:half], refs[half:]):
        norm_kernel(src, dst)


def normalize_each(*arrays, us=0.6):
    return pl.pallas_call(
        norm_each_kernel,
        out_shape=tuple(sds(a.shape, BF16) for a in arrays),
        in_specs=[VM] * len(arrays),
        out_specs=tuple([VM] * len(arrays)),
        compiler_params=PARAMS,
        cost_estimate=cost(us),
        name="normalize_each",
    )(*fast(*arrays))


def normalize(*pieces, us=0.8):
    rows = sum(p.shape[0] for p in pieces)
    width = pieces[0].shape[1]
    return pl.pallas_call(
        norm_kernel,
        out_shape=sds((rows, width), BF16),
        in_specs=[VM] * len(pieces),
        out_specs=VM,
        compiler_params=PARAMS,
        cost_estimate=cost(us),
        name="normalize",
    )(*fast(*pieces))


def setup(tab, scale, own, across):
    return pl.pallas_call(
        setup_kernel,
        out_shape=(sds((4, 256), jnp.int32), sds((1024, 128), jnp.int32), sds((8, 128), F32)),
        in_specs=[SM, SM, VM, VM],
        out_specs=(VM, VM, VM),
        compiler_params=PARAMS,
        cost_estimate=cost(1),
        name="setup",
    )(tab, scale, own, across)


def tile(quarter, weight, pos, ids, xh, yh):
    return pl.pallas_call(
        functools.partial(tile_kernel, quarter),
        out_shape=sds((yh.shape[0], xh.shape[0]), BF16),
        in_specs=[VM] * 5,
        out_specs=VM,
        compiler_params=PARAMS,
        cost_estimate=cost(1.3),
        name="tile",
    )(*fast(weight, pos, ids, xh, yh))


def image_sum(raw, yh, g):
    return pl.pallas_call(
        image_kernel,
        out_shape=sds(raw.shape, BF16),
        in_specs=[VM] * 3,
        out_specs=VM,
        scratch_shapes=[pltpu.VMEM(raw.shape, F32)],
        compiler_params=PARAMS,
        cost_estimate=cost(1.6),
        name="image_sum",
    )(*fast(raw, yh, g))


def text_sum(first, gs, xs, pieces, name):
    arrays = [p[0] for p in pieces]
    spans = tuple((low, high) for _, low, high in pieces)
    rows = sum(high - low for low, high in spans)
    width = arrays[0].shape[1]
    return pl.pallas_call(
        functools.partial(text_kernel, first, spans),
        out_shape=sds((rows, width), BF16),
        in_specs=[VM] * (8 + len(arrays)),
        out_specs=VM,
        scratch_shapes=[pltpu.VMEM((rows, width), F32)],
        compiler_params=PARAMS,
        cost_estimate=cost(rows / 230),
        name=name,
    )(*fast(*gs, *xs, *arrays))


def add(*terms):
    total = terms[0].astype(F32)
    for t in terms[1:]:
        total = total + t.astype(F32)
    return total


def local(image_emb, text_emb, positive, loss_scale):
    i, t = lax.axis_index("img"), lax.axis_index("txt")
    z, yh = i // 2, i % 2
    yl, x, c = t // 8, (t // 2) % 4, t % 2
    y = yh * 2 + yl
    s = 1 - 2 * c
    d = 1 - c

    other = send(text_emb, CORE)
    images, text_emb = fetch(image_emb, text_emb)
    chip = join(text_emb, other)
    one = send(chip, Z_ONE)
    two = send(chip, Z_TWO)
    three = send(two, Z_ONE)
    four = send(head(two, 64), Z_TWO)

    def text_base(zz, cc):
        return ((((yl * 4 + x) * 2 + cc) * 8 + zz % 8) * 2 + yh) * 64

    at = [(z - 3 * s, c), (z - 3 * s, d), (z + 4, c)]
    at += [(z - s, c), (z - s, d), (z - 2 * s, c), (z - 2 * s, d), (z, d)]
    at += [(z + 3 * s, d), (z + 3 * s, c), (z + 4, d)]
    at += [(z + s, d), (z + s, c), (z + 2 * s, d), (z + 2 * s, c), (z, c)]
    table = [text_base(*p) for p in at]
    rows, mine = [], []
    for b in (0, -1, 1, 2):
        for a in (0, -1, 1, 2):
            yy = (y + jnp.where(c == 0, b, a)) % 4
            xx = (x + jnp.where(c == 0, a, b)) % 4
            rows.append(yy % 2 * 4 + xx)
            mine.append((yy // 2 == yh).astype(jnp.int32))
    tab = jnp.stack([v.astype(jnp.int32) for v in table + rows + mine + [c]])
    scale = (loss_scale * (temper / 16384.0)).reshape(1)
    own_pairs = positive.reshape(8, 128)
    own_pairs, three = lax.optimization_barrier((own_pairs, three))
    across_pairs = send(own_pairs, Y_TWO)
    pos, ids, weight = setup(tab, scale, own_pairs, across_pairs)

    give = join(three, four, one, two)
    keep = send(give, CORE)
    far_give, near_give = [(give, 0, 192)], [(give, 192, 448), (other, 0, 64)]
    far_keep, near_keep = [(keep, 0, 192)], [(keep, 192, 448), (text_emb, 0, 64)]

    row = join(images, send(image_emb, A_ON), send(image_emb, A_BACK), send(image_emb, A_TWO))
    quarters = [row, send(row, B_ON), send(row, B_BACK), send(row, B_TWO)]

    yh_all = normalize(give, other, keep, text_emb)
    xs, gs = [None] * 4, [None] * 4
    xs[0] = normalize(quarters[0], us=0.3)
    xs[2], xs[3] = normalize_each(quarters[2], quarters[3], us=100)
    for k in (0, 2, 3):
        gs[k] = tile(k, weight, pos, ids, xs[k], yh_all)
    quarters[1], gs[0], gs[2], gs[3] = lax.optimization_barrier((quarters[1], gs[0], gs[2], gs[3]))
    xs[1] = normalize(quarters[1], us=20)
    gs[1] = tile(1, weight, pos, ids, xs[1], yh_all)
    d_give = text_sum(0, gs, xs, far_give, "far_give")
    swapped = send(d_give, CORE)
    d_keep = text_sum(512, gs, xs, far_keep, "far_keep")
    far_sum = add(d_keep, swapped).astype(BF16)
    relay = send(far_sum, Z_TWO)

    far_sum, *gs = lax.optimization_barrier((far_sum, *gs))
    es = [image_sum(quarters[k], yh_all, gs[k]) for k in range(4)]
    back = [send(es[1], B_BACK), send(es[2], B_ON), send(es[3], B_TWO)]

    _, *gs = lax.optimization_barrier((es[3], *gs))
    d_give = text_sum(192, gs, xs, near_give, "near_give")
    swapped = send(d_give, CORE)
    d_keep = text_sum(704, gs, xs, near_keep, "near_keep")
    near_sum = add(d_keep, swapped)
    (relay,) = fetch(relay, us=40)
    half = add(near_sum[0:192], relay).astype(BF16)
    own_sum, half = lax.optimization_barrier((es[0], half))
    row_sum = add(own_sum, *back)
    row_half = row_sum.astype(BF16)
    home = [send(row_half[64:128], A_BACK), send(row_half[128:192], A_ON), send(row_half[192:256], A_TWO)]
    grad_image = add(row_sum[:64], *home).astype(BF16)

    w1 = send(half[0:128], Z_ONE)
    w2 = send(jnp.concatenate([half[128:192], near_sum[192:256].astype(BF16)], axis=0), Z_TWO)
    w1, w2 = fetch(w1, w2, us=40)
    to_other = add(w1[:64], w2[:64]).astype(BF16)
    last = send(to_other, CORE)
    grad_text = add(near_sum[256:320], w1[64:], w2[64:], last).astype(BF16)
    return grad_image, grad_text


def solution(mesh):
    in_specs = (P(("img", "txt"), None), P(("txt", "img"), None), P("img"), P())
    out_specs = (P(("img", "txt"), None), P(("txt", "img"), None))
    return jax.shard_map(local, mesh=mesh, in_specs=in_specs, out_specs=out_specs, check_vma=False)
```
